32 devices in a mesh: dp: 4 (over z), expert: 8 (over y, x, core).
Axes of the slice: x: 2, y: 2, z: 4, core: 2. Of those that a mesh axis runs over, the one named last changes fastest.
Arguments:
- tokens: bfloat16 [4096, 1664], P(('dp', 'expert')), may hold values from -6 to 6
- cotangent: bfloat16 [4096, 1664], P(('dp', 'expert')), may hold values from -6 to 6
- counts: int32 [4096], P(('dp', 'expert')), may hold values from 0 to 8
- picks: int32 [4, 8, 8], P('dp'), may hold values from 0 to 1023, as said below
- router: float32 [1664, 8], replicated, may hold values from -1 to 1
- w_in: bfloat16 [8, 1664, 4096], P('expert', None, 'dp'), may hold values from -0.15625 to 0.15625
- w_out: bfloat16 [8, 4096, 1664], P('expert', 'dp'), may hold values from -0.09375 to 0.09375
Outputs:
- grad_tokens: bfloat16 [4096, 1664], P(('dp', 'expert'))
- grad_w_in: bfloat16 [8, 1664, 4096], P('expert', None, 'dp')
- grad_w_out: bfloat16 [8, 4096, 1664], P('expert', 'dp')
- grad_router: float32 [1664, 8], replicated
The draws below stay inside these ranges and needn't reach their ends.
Inputs may be any that keep to these rules, and one draw needn't show every extreme that they name: For each group and each expert, 8 distinct positions in increasing order; positions k * 128 to (k + 1) * 128 - 1 hold at most 2 of one expert's picks, and each expert takes exactly 2 from some such range in every group.
All inputs are finite; a program needn't handle non-finite values.
Results may differ from the reference program's by a relative error of at most 0.017.
Values may be sent and summed in bfloat16 or wider, within the bound.
A program may use at most 64 MiB of HBM per device.

```python
import math
import jax
import jax.numpy as jnp
from jax import lax

D = 1664
FFN = 4096
SLOT = 2
TOK_DEV = 128
EXPERTS = 8
GROUP = 1024
GROUPS = 4
TOKENS = 4096
CAP = 8
N_EXPERT = 8


def draw_router(key, part):
    normal = jax.random.normal(jax.random.fold_in(key, 3), (D, EXPERTS), jnp.float32) * (2.0 / math.sqrt(D))
    normal = jnp.clip(normal, -1.0, 1.0)
    return normal


def draw_tokens(key, part):
    values = jnp.clip(jax.random.normal(jax.random.fold_in(key, 5), (TOKENS, D), jnp.float32), -6.0, 6.0)
    positions = jnp.arange(TOKENS)
    device_of = positions // TOK_DEV
    device_sign = jnp.where(jax.random.bernoulli(jax.random.fold_in(key, 11), 0.5, (TOKENS // TOK_DEV,)), 5.0, -5.0)
    spike_col = device_of % D
    columns = jnp.arange(D)
    values = jnp.where(columns[None, :] == spike_col[:, None], device_sign[device_of][:, None], values)
    return values.astype(jnp.bfloat16)


def pick_plan(key):
    base_key = jax.random.fold_in(key, 29)
    forced_count = min(8, EXPERTS)

    def one_group(group_key):
        key_perm, key_amount, key_order = jax.random.split(group_key, 3)
        perms = jax.vmap(lambda sub_key: jax.random.permutation(sub_key, N_EXPERT))(jax.random.split(key_perm, EXPERTS))
        column_ids = jnp.arange(N_EXPERT, dtype=perms.dtype)
        swapped = jnp.where(perms == 0, perms[:, 0:1], jnp.where(column_ids[None, :] == 0, 0, perms))
        forced = jnp.arange(EXPERTS)[:, None] < forced_count
        perms = jnp.where(forced, swapped, perms)
        half_count = N_EXPERT // 2
        amount = jax.random.randint(key_amount, (EXPERTS, half_count), 0, SLOT + 1)
        amount = amount.at[:, 0].set(SLOT)
        paired = jnp.concatenate([amount, SLOT - amount], axis=1)
        inverse = jnp.argsort(perms, axis=1, stable=True)
        per_source = jnp.take_along_axis(paired, inverse, axis=1)
        source_total = jnp.sum(per_source, axis=0)
        window = jnp.minimum(jnp.maximum(SLOT, (source_total + 7) // 8), TOK_DEV)
        starts = jnp.cumsum(per_source, axis=0) - per_source
        orders = jax.vmap(lambda sub_key: jax.random.permutation(sub_key, TOK_DEV))(jax.random.split(key_order, N_EXPERT))
        slot_rank = jnp.arange(SLOT, dtype=jnp.int32)
        sources = jnp.arange(N_EXPERT, dtype=jnp.int32)
        position = (starts[:, :, None] + slot_rank[None, None, :]) % window[None, :, None]
        local_pos = orders[sources[None, :, None], position]
        special = orders[0, TOK_DEV - 1]
        special_mask = forced[:, :, None] & (sources[None, :, None] == 0) & (slot_rank[None, None, :] == 0)
        local_pos = jnp.where(special_mask, special, local_pos)
        valid = slot_rank[None, None, :] < per_source[:, :, None]
        code = jnp.where(valid, sources[None, :, None] * TOK_DEV + local_pos, GROUP)
        ranked = jnp.sort(code.reshape(EXPERTS, N_EXPERT * SLOT), axis=1)[:, :CAP]
        tally = jnp.zeros((GROUP,), jnp.int32).at[ranked.reshape(-1)].add(1)
        return (ranked.astype(jnp.int32), tally)
    plans, tallies = jax.vmap(one_group)(jax.random.split(base_key, GROUPS))
    return (plans, tallies.reshape(-1))


def draw_picks(key, part):
    return pick_plan(key)[0]


def draw_counts(key, part):
    return pick_plan(key)[1]


def block_levels(own_key, dims, pieces, smallest, high):
    factor_of = 1.0
    for dim, parts in pieces:
        heights = jax.random.uniform(jax.random.fold_in(jax.random.fold_in(own_key, 6), dim), (parts,), jnp.float32, smallest / len(pieces), high / len(pieces))
        factor_of = factor_of * jnp.repeat(jnp.exp(heights), dims[dim] // parts).reshape((-1,) + (1,) * (len(dims) - 1 - dim))
    return factor_of


def gaussian(rng, shape, deviation, limit, shards=(), kind=jnp.bfloat16):
    level = block_levels(rng, shape, shards, -0.22, 0.18) if shards else 1.0
    array = jax.random.normal(rng, shape, jnp.float32) * deviation * level
    return jnp.minimum(jnp.maximum(array, -limit), limit).astype(kind)


def setup_inputs(seed: int = 0) -> dict:
    seeds = jax.random.split(jax.random.key(seed), 8)
    return {
        "tokens": draw_tokens(jax.random.fold_in(seeds[7], 71), 0),
        "cotangent": gaussian(seeds[1], (TOKENS, D), 1.0, 6.0, ((0, 32),)),
        "counts": draw_counts(jax.random.fold_in(seeds[7], 71), 0),
        "picks": draw_picks(jax.random.fold_in(seeds[7], 71), 0),
        "router": draw_router(jax.random.fold_in(seeds[7], 71), 0),
        "w_in": gaussian(seeds[5], (EXPERTS, D, FFN), D ** -0.5, 0.15625, ((0, 8), (2, 4))),
        "w_out": gaussian(seeds[6], (EXPERTS, FFN, D), FFN ** -0.5, 0.09375, ((0, 8), (1, 4))),
    }


def normal_cdf(values):
    return 0.5 * (1.0 + jax.scipy.special.erf(values * 0.7071067811865476))


def gelu_exact(values):
    return values * normal_cdf(values)


def gelu_slope(values):
    return normal_cdf(values) + values * jnp.exp(-0.5 * values * values) * 0.3989422804014327


def reference(tokens, cotangent, counts, picks, router, w_in, w_out):
    tokens_wide = tokens.astype(jnp.float32)
    logits = jnp.dot(tokens_wide, router, precision=lax.Precision.HIGHEST)
    router_prob = jax.nn.softmax(logits, axis=-1)
    weight = jnp.maximum(counts, 1).astype(jnp.float32)
    scaled = (cotangent.astype(jnp.float32) / weight[:, None]).astype(jnp.bfloat16)
    offsets = (jnp.arange(GROUPS, dtype=jnp.int32) * GROUP).astype(jnp.int32)
    pick_rows = (picks + offsets[:, None, None]).astype(jnp.int32)
    rows_by_expert = jnp.transpose(pick_rows, (1, 0, 2)).reshape(EXPERTS, GROUPS * CAP)
    block_width = FFN // GROUPS

    def per_expert(operands):
        row_index, mat_in, mat_out, expert_id = operands
        rows_x = tokens[row_index]
        rows_dy = scaled[row_index]
        gate = router_prob[row_index, expert_id].astype(jnp.bfloat16)
        pre_act = jnp.dot(rows_x, mat_in, preferred_element_type=jnp.float32)
        activated = gelu_exact(pre_act).astype(jnp.bfloat16)
        out_grad = (gate.astype(jnp.float32)[:, None] * rows_dy.astype(jnp.float32)).astype(jnp.bfloat16)
        grad_out = jnp.dot(activated.T, out_grad, preferred_element_type=jnp.float32).astype(jnp.bfloat16)
        act_grad = jnp.dot(out_grad, mat_out.T, preferred_element_type=jnp.float32)
        pre_grad = (act_grad * gelu_slope(pre_act)).astype(jnp.bfloat16)
        grad_in = jnp.dot(rows_x.T, pre_grad, preferred_element_type=jnp.float32).astype(jnp.bfloat16)
        row_sum = jnp.zeros((rows_x.shape[0], D), jnp.float32)
        gate_sum = jnp.zeros((rows_x.shape[0],), jnp.float32)
        dy_wide = rows_dy.astype(jnp.float32)
        for block_id in range(GROUPS):
            low_col = block_id * block_width
            high_col = low_col + block_width
            part_out = jnp.dot(activated[:, low_col:high_col], mat_out[low_col:high_col], preferred_element_type=jnp.float32)
            gate_sum = gate_sum + jnp.sum(dy_wide * part_out, axis=-1)
            row_part = jnp.dot(pre_grad[:, low_col:high_col], mat_in[:, low_col:high_col].T, preferred_element_type=jnp.float32)
            row_part = lax.optimization_barrier(row_part.astype(jnp.bfloat16))
            row_sum = row_sum + row_part.astype(jnp.float32)
        return grad_in, grad_out, row_sum.astype(jnp.bfloat16), gate_sum.astype(jnp.bfloat16)

    grad_w_in, grad_w_out, row_grad, gate_grad = lax.map(per_expert, (rows_by_expert, w_in, w_out, jnp.arange(EXPERTS, dtype=jnp.int32)))
    flat_rows = rows_by_expert.reshape(-1)
    expert_cols = jnp.repeat(jnp.arange(EXPERTS, dtype=jnp.int32), GROUPS * CAP)
    expert_sum = jnp.zeros((TOKENS, D), jnp.float32).at[flat_rows].add(row_grad.reshape(-1, D).astype(jnp.float32))
    prob_grad = jnp.zeros((TOKENS, EXPERTS), jnp.float32).at[flat_rows, expert_cols].add(gate_grad.reshape(-1).astype(jnp.float32))
    logit_grad = router_prob * (prob_grad - jnp.sum(router_prob * prob_grad, axis=-1, keepdims=True))
    grad_tokens = (expert_sum + jnp.dot(logit_grad, router.T, precision=lax.Precision.HIGHEST)).astype(jnp.bfloat16)
    grad_router = jnp.dot(tokens_wide.T, logit_grad, precision=lax.Precision.HIGHEST)
    return (grad_tokens, grad_w_in, grad_w_out, grad_router)
```

```python
import functools

import jax
import jax.numpy as jnp
from jax import lax
from jax.experimental import pallas as pl
from jax.experimental.pallas import tpu as pltpu
from jax.sharding import PartitionSpec as P

MESH = pl.DeviceIdType.MESH
BF16 = jnp.bfloat16
F32 = jnp.float32
SLOT = 2
SEG = 16
LANES = 128


def nn(left, right):
    return lax.dot_general(left, right, (((1,), (0,)), ((), ())), preferred_element_type=F32)


def nt(left, right):
    return lax.dot_general(left, right, (((1,), (1,)), ((), ())), preferred_element_type=F32)


def tn(left, right):
    return lax.dot_general(left, right, (((0,), (0,)), ((), ())), preferred_element_type=F32)


def iota(shape, dim):
    return lax.broadcasted_iota(jnp.int32, shape, dim)


def one_hot(mask):
    return jnp.where(mask, 1.0, 0.0).astype(BF16)


def split3(values):
    high = values.astype(BF16).astype(F32)
    rest = values - high
    mid = rest.astype(BF16).astype(F32)
    return high, mid, rest - mid


def normal_cdf(values):
    return 0.5 * (1.0 + lax.erf(values * 0.7071067811865476))


def exchange(axis, count, me, source, target, send_sem, recv_sem):
    copies = []
    for step in range(1, count):
        peer = lax.rem(me + step, count)
        copy = pltpu.make_async_remote_copy(
            src_ref=source(peer),
            dst_ref=target,
            send_sem=send_sem.at[step],
            recv_sem=recv_sem.at[step],
            device_id={axis: peer},
            device_id_type=MESH,
        )
        copy.start()
        copies.append(copy)
    return copies


def arrive(copies):
    for copy in copies:
        copy.wait_recv()


def route_kernel(
    experts, groups, tok_ref, cot_ref, cnt_ref, pick_ref, router_ref, win_hbm, wout_hbm,
    x_ref, og_ref, act_ref, pg_ref, gt_ref, gr_ref,
    win, wout, send, recv, pack, acc, rows_s, rows_r, gate_r, gate_s, gates, ret_s, ret_r,
    term_s, term_r, sum_r, fin_r,
    w_sem, d_ss, d_rs, p_ss, p_rs, g_ss, g_rs, e_ss, e_rs, r_ss, r_rs, b_ss, b_rs,
    t_ss, t_rs, s_ss, s_rs, f_ss, f_rs,
):
    me = lax.axis_index("expert")
    my_group = lax.axis_index("dp")
    toks, width = tok_ref.shape
    capacity = pick_ref.shape[1]
    hidden = win.shape[1]
    count = groups * capacity
    piece = send.shape[2]
    half = rows_s.shape[2]
    back = ret_s.shape[2]
    chunk = term_s.shape[2]

    barrier = pltpu.get_barrier_semaphore()
    for step in range(1, experts):
        pl.semaphore_signal(
            barrier, inc=1, device_id={"expert": lax.rem(me + step, experts)}, device_id_type=MESH
        )
    for step in range(1, groups):
        pl.semaphore_signal(
            barrier, inc=1, device_id={"dp": lax.rem(my_group + step, groups)}, device_id_type=MESH
        )
    load_in = pltpu.make_async_copy(win_hbm, win, w_sem.at[0])
    load_out = pltpu.make_async_copy(wout_hbm, wout, w_sem.at[1])
    load_in.start()
    load_out.start()

    tok = tok_ref[...]
    router = router_ref[...]
    stacked = jnp.concatenate(split3(router), axis=0).astype(BF16)
    parts = nt(stacked, tok)
    logits = parts[:experts] + parts[experts : 2 * experts] + parts[2 * experts :]
    raised = jnp.exp(logits - jnp.max(logits, axis=0, keepdims=True))
    prob = raised / jnp.sum(raised, axis=0, keepdims=True)
    weight_row = jnp.maximum(cnt_ref[...], 1).astype(F32)
    diagonal = iota((toks, toks), 0) == iota((toks, toks), 1)
    weight = jnp.sum(jnp.where(diagonal, weight_row, 0.0), axis=1, keepdims=True)
    scaled = (cot_ref[...].astype(F32) / weight).astype(BF16)

    picks = pick_ref[...]
    owner = picks // toks
    place = picks - owner * toks
    codes = jnp.concatenate([owner, place], axis=1).astype(F32).astype(BF16)
    wide = experts * SEG
    spread = one_hot(iota((wide, experts), 0) // SEG == iota((wide, experts), 1))
    spread_codes = nn(spread, codes)
    held = spread_codes[:, :capacity] == me.astype(F32)
    spots = spread_codes[:, capacity:]
    first = jnp.min(jnp.where(held, spots, 1e6), axis=1, keepdims=True)
    last = jnp.max(jnp.where(held, spots, -1.0), axis=1, keepdims=True)
    last = jnp.where(last > first, last, -1.0)
    seat = iota((wide, toks), 0) % SEG
    token_id = iota((wide, toks), 1).astype(F32)
    hit = (token_id == jnp.where(seat % SLOT == 0, first, last)).astype(F32)

    pieces = SEG // (2 * SLOT)
    total = jnp.zeros((wide, piece), F32)
    for part in range(pieces):
        low = part * piece
        high = min(width, low + piece)
        inside = seat // (2 * SLOT) == part
        late = seat % (2 * SLOT) >= SLOT
        take_x = jnp.where(inside & ~late, hit, 0.0).astype(BF16)
        take_dy = jnp.where(inside & late, hit, 0.0).astype(BF16)
        term = nn(take_x, tok[:, low:high]) + nn(take_dy, scaled[:, low:high])
        if part == pieces - 1:
            padded = jnp.concatenate([prob, jnp.zeros((LANES - experts, toks), F32)], axis=0)
            gate_cols = nt(take_dy, padded.astype(BF16))
            columns = [term, gate_cols]
            spare = piece - (high - low) - LANES
            if spare:
                columns.append(jnp.zeros((wide, spare), F32))
            term = jnp.concatenate(columns, axis=1)
        total = total + term
    send[...] = total.astype(BF16).reshape(experts, SEG, piece)
    recv[pl.ds(me, 1)] = send[pl.ds(me, 1)]

    pl.semaphore_wait(barrier, experts - 1 + groups - 1)
    dispatch = exchange("expert", experts, me, lambda peer: send.at[peer], recv.at[me], d_ss, d_rs)

    mine = iota((experts, capacity), 0) == me
    owner_row = jnp.sum(jnp.where(mine, owner, 0), axis=0, keepdims=True)
    tall = 2 * capacity
    slot_row = iota((tall, capacity), 0) % capacity
    slot_col = iota((tall, capacity), 1)
    owner_col = jnp.sum(jnp.where(slot_row == slot_col, owner_row, 0), axis=1, keepdims=True)
    same = owner_col == owner_row
    rank_col = jnp.sum(jnp.where(same & (slot_col < slot_row), 1, 0), axis=1, keepdims=True)
    seat_c = iota((tall, wide), 1) % SEG
    is_dy = jnp.where(iota((tall, wide), 0) >= capacity, 1, 0)
    wanted = (iota((tall, wide), 1) // SEG == owner_col) & (
        seat_c % (2 * SLOT) == SLOT * is_dy + rank_col
    )
    before = same[:capacity] & (slot_row[:capacity] < slot_col[:capacity])
    rank_row = jnp.sum(jnp.where(before, 1, 0), axis=0, keepdims=True)
    row_u = iota((wide, capacity), 0)
    from_owner = row_u // SEG == owner_row

    arrive(dispatch)
    rows_in = recv[...].reshape(wide, piece)
    packed = []
    for part in range(pieces):
        block = one_hot(wanted & (seat_c // (2 * SLOT) == part))
        packed.append(nn(block, rows_in).astype(BF16))
    whole = pack.shape[2]
    for part in range(pieces):
        low = part * piece
        high = min(whole, low + piece)
        pack[pl.ds(my_group, 1), :, low:high] = packed[part][None, :, : high - low]
    gather = exchange("dp", groups, my_group, lambda peer: pack.at[my_group], pack.at[my_group], p_ss, p_rs)
    arrive(gather)

    every = pack[...].astype(F32)
    x_rows = every[:, :capacity, :width].reshape(count, width).astype(BF16)
    dy_wide = every[:, capacity:, :width].reshape(count, width)
    gate_lanes = every[:, capacity:, width : width + LANES].reshape(count, LANES)
    lane = iota((count, LANES), 1)
    gate = jnp.sum(jnp.where(lane == me, gate_lanes, 0.0), axis=1, keepdims=True)
    dy_rows = dy_wide.astype(BF16)
    x_ref[...] = x_rows
    og_ref[...] = (gate * dy_wide).astype(BF16)

    load_in.wait()
    load_out.wait()
    step_cols = min(hidden, 256)
    gate_part = jnp.zeros((count, 1), F32)
    for tile in range(hidden // step_cols):
        cols = slice(tile * step_cols, (tile + 1) * step_cols)
        pre = nn(x_rows, win[:, cols])
        back_act = nt(dy_rows, wout[cols, :])
        cdf = normal_cdf(pre)
        act = (pre * cdf).astype(BF16)
        slope = cdf + pre * jnp.exp(-0.5 * pre * pre) * 0.3989422804014327
        act_ref[:, cols] = act
        pg_ref[:, cols] = (gate * back_act * slope).astype(BF16)
        gate_part = gate_part + jnp.sum(act.astype(F32) * back_act, axis=1, keepdims=True)
    gate_s[...] = jnp.broadcast_to(gate_part, (count, LANES)).reshape(groups, capacity, LANES)
    gate_r[pl.ds(my_group, 1)] = gate_s[pl.ds(my_group, 1)]
    gate_sum = exchange("dp", groups, my_group, lambda peer: gate_s.at[peer], gate_r.at[my_group], g_ss, g_rs)

    for tile in range(hidden // step_cols):
        cols = slice(tile * step_cols, (tile + 1) * step_cols)
        term = nt(pg_ref[:, cols], win[:, cols])
        if tile == 0:
            acc[...] = term
        else:
            acc[...] += term
    row_part = acc[...].reshape(groups, capacity, width)
    right = jnp.concatenate(
        [row_part[:, :, half:], jnp.zeros((groups, capacity, 2 * half - width), F32)], axis=2
    )
    rows_s[...] = jnp.concatenate([row_part[:, :, :half], right], axis=1).astype(BF16)
    rows_r[pl.ds(my_group, 1)] = rows_s[pl.ds(my_group, 1)]
    row_sum = exchange("dp", groups, my_group, lambda peer: rows_s.at[peer], rows_r.at[my_group], r_ss, r_rs)

    arrive(gate_sum)
    gate_total = gate_r[0]
    for group in range(1, groups):
        gate_total = gate_total + gate_r[group]
    gate_total = gate_total.astype(BF16).astype(F32)
    gate_total = jnp.where(iota((capacity, LANES), 1) == me, gate_total, 0.0)
    gates[pl.ds(me, 1)] = gate_total[None]
    gate_back = exchange("expert", experts, me, lambda peer: gates.at[me], gates.at[me], e_ss, e_rs)

    arrive(row_sum)
    row_total = rows_r[0].astype(F32)
    for group in range(1, groups):
        row_total = row_total + rows_r[group].astype(F32)
    row_grad = jnp.concatenate(
        [row_total[:capacity], row_total[capacity:, : width - half]], axis=1
    ).astype(BF16).astype(F32)
    returned = jnp.zeros((wide, back), F32)
    back_pieces = SEG // SLOT
    for part in range(back_pieces):
        low = part * back
        high = min(width, low + back)
        if high <= low:
            continue
        give = jnp.where(from_owner & (row_u % SEG == SLOT * part + rank_row), 1.0, 0.0)
        term = nn(give, row_grad[:, low:high])
        if high - low < back:
            term = jnp.concatenate([term, jnp.zeros((wide, back - high + low), F32)], axis=1)
        returned = returned + term
    ret_s[...] = returned.astype(BF16).reshape(experts, SEG, back)
    ret_r[pl.ds(me, 1)] = ret_s[pl.ds(me, 1)]
    give_back = exchange("expert", experts, me, lambda peer: ret_s.at[peer], ret_r.at[me], b_ss, b_rs)

    flat = experts * capacity
    spread_c = one_hot(iota((flat, experts), 0) // capacity == iota((flat, experts), 1))
    flat_codes = nn(spread_c, codes)
    own_pick = (iota((flat, capacity), 0) % capacity == iota((flat, capacity), 1)) & (
        flat_codes[:, :capacity] == me.astype(F32)
    )
    spot = jnp.sum(jnp.where(own_pick, flat_codes[:, capacity:] + 1.0, 0.0), axis=1, keepdims=True)
    at_token = one_hot(iota((flat, toks), 1).astype(F32) + 1.0 == spot)
    arrive(gate_back)
    gate_rows = gates[...].reshape(flat, LANES).astype(BF16)
    prob_grad = tn(gate_rows, at_token)[:experts]
    logit_grad = prob * (prob_grad - jnp.sum(prob * prob_grad, axis=0, keepdims=True))
    lg3 = jnp.concatenate(split3(logit_grad), axis=0).astype(BF16)
    terms = nn(lg3, tok)
    term = terms[:experts] + terms[experts : 2 * experts] + terms[2 * experts :]
    for part in range(experts):
        low = part * chunk
        high = min(width, low + chunk)
        if high <= low:
            term_s[part] = jnp.zeros((experts, chunk), F32)
            continue
        value = term[:, low:high]
        if high - low < chunk:
            value = jnp.concatenate([value, jnp.zeros((experts, chunk - high + low), F32)], axis=1)
        term_s[part] = value
    term_r[pl.ds(me, 1)] = term_s[pl.ds(me, 1)]
    scatter = exchange("expert", experts, me, lambda peer: term_s.at[peer], term_r.at[me], t_ss, t_rs)

    r1, r2, r3 = split3(router)
    l1, l2, l3 = split3(logit_grad)
    left = jnp.concatenate([l1, l1, l2, l1, l3, l2], axis=0).astype(BF16)
    near = jnp.concatenate([r1, r2, r1, r3, r1, r2], axis=0).astype(BF16)
    gt_wide = tn(left, near)

    arrive(scatter)
    term_sum = term_r[0]
    for part in range(1, experts):
        term_sum = term_sum + term_r[part]
    sum_r[pl.ds(my_group, 1)] = term_sum[None]
    over_dp = exchange("dp", groups, my_group, lambda peer: sum_r.at[my_group], sum_r.at[my_group], s_ss, s_rs)

    arrive(give_back)
    ret_rows = ret_r[...].reshape(wide, back)
    for part in range(back_pieces):
        low = part * back
        high = min(width, low + back)
        if high <= low:
            continue
        mark = jnp.where(seat // SLOT == part, hit, 0.0).astype(BF16)
        expert_sum = tn(mark, ret_rows[:, : high - low])
        gt_ref[:, low:high] = (expert_sum + gt_wide[:, low:high]).astype(BF16)

    arrive(over_dp)
    final = sum_r[0]
    for group in range(1, groups):
        final = final + sum_r[group]
    fin_r[pl.ds(me, 1)] = final[None]
    spread_out = exchange("expert", experts, me, lambda peer: fin_r.at[me], fin_r.at[me], f_ss, f_rs)
    arrive(spread_out)
    for part in range(experts):
        low = part * chunk
        high = min(width, low + chunk)
        if high > low:
            gr_ref[:, low:high] = fin_r[part][:, : high - low]
    for copies in (
        dispatch, gather, gate_sum, row_sum, gate_back, give_back, scatter, over_dp, spread_out
    ):
        for copy in copies:
            copy.wait_send()


def weight_kernel(x_ref, og_ref, act_ref, pg_ref, gin_ref, gout_ref):
    gin_ref[0] = tn(x_ref[...], pg_ref[...]).astype(BF16)
    gout_ref[0] = tn(act_ref[...], og_ref[...]).astype(BF16)


def shards(experts, groups, tokens, cotangent, counts, picks, router, w_in, w_out):
    toks, width = tokens.shape
    capacity = picks.shape[2]
    hidden = w_in.shape[2]
    count = groups * capacity
    tiles = -(-width // LANES)
    pieces = SEG // (2 * SLOT)
    piece = LANES * -(-(tiles + 1) // pieces)
    whole = width + LANES
    half = LANES * -(-tiles // 2)
    back = LANES * -(-tiles // (SEG // SLOT))
    chunk = LANES * -(-tiles // experts)
    vmem = pl.BlockSpec(memory_space=pltpu.VMEM)
    hbm = pl.BlockSpec(memory_space=pl.ANY)
    dma = pltpu.SemaphoreType.DMA
    over_e, over_g = dma((experts,)), dma((groups,))
    x_rows, out_grad, act, pre_grad, grad_tokens, grad_router = pl.pallas_call(
        functools.partial(route_kernel, experts, groups),
        out_shape=(
            jax.ShapeDtypeStruct((count, width), BF16),
            jax.ShapeDtypeStruct((count, width), BF16),
            jax.ShapeDtypeStruct((count, hidden), BF16),
            jax.ShapeDtypeStruct((count, hidden), BF16),
            jax.ShapeDtypeStruct((toks, width), BF16),
            jax.ShapeDtypeStruct((experts, width), F32),
        ),
        in_specs=[vmem] * 5 + [hbm] * 2,
        out_specs=(vmem,) * 6,
        scratch_shapes=[
            pltpu.VMEM((width, hidden), BF16),
            pltpu.VMEM((hidden, width), BF16),
            pltpu.VMEM((experts, SEG, piece), BF16),
            pltpu.VMEM((experts, SEG, piece), BF16),
            pltpu.VMEM((groups, 2 * capacity, whole), BF16),
            pltpu.VMEM((count, width), F32),
            pltpu.VMEM((groups, 2 * capacity, half), BF16),
            pltpu.VMEM((groups, 2 * capacity, half), BF16),
            pltpu.VMEM((groups, capacity, LANES), F32),
            pltpu.VMEM((groups, capacity, LANES), F32),
            pltpu.VMEM((experts, capacity, LANES), F32),
            pltpu.VMEM((experts, SEG, back), BF16),
            pltpu.VMEM((experts, SEG, back), BF16),
            pltpu.VMEM((experts, experts, chunk), F32),
            pltpu.VMEM((experts, experts, chunk), F32),
            pltpu.VMEM((groups, experts, chunk), F32),
            pltpu.VMEM((experts, experts, chunk), F32),
            dma((2,)),
            over_e, over_e,
            over_g, over_g,
            over_g, over_g,
            over_e, over_e,
            over_g, over_g,
            over_e, over_e,
            over_e, over_e,
            over_g, over_g,
            over_e, over_e,
        ],
        compiler_params=pltpu.CompilerParams(
            collective_id=0, has_side_effects=True, vmem_limit_bytes=48 * 1024 * 1024
        ),
        name="route",
    )(tokens, cotangent, counts.reshape(1, toks), picks[0], router.T, w_in[0], w_out[0])

    cols = min(hidden, 256)
    grad_in, grad_out = pl.pallas_call(
        weight_kernel,
        grid=(hidden // cols,),
        out_shape=(
            jax.ShapeDtypeStruct((1, width, hidden), BF16),
            jax.ShapeDtypeStruct((1, hidden, width), BF16),
        ),
        in_specs=[
            pl.BlockSpec((count, width), lambda i: (0, 0)),
            pl.BlockSpec((count, width), lambda i: (0, 0)),
            pl.BlockSpec((count, cols), lambda i: (0, i)),
            pl.BlockSpec((count, cols), lambda i: (0, i)),
        ],
        out_specs=(
            pl.BlockSpec((1, width, cols), lambda i: (0, 0, i)),
            pl.BlockSpec((1, cols, width), lambda i: (0, i, 0)),
        ),
        compiler_params=pltpu.CompilerParams(vmem_limit_bytes=32 * 1024 * 1024),
        name="weight_grads",
    )(x_rows, out_grad, act, pre_grad)
    return grad_tokens, grad_in, grad_out, grad_router.T


def solution(mesh):
    placed = (
        P(("dp", "expert"), None),
        P(("dp", "expert"), None),
        P(("dp", "expert")),
        P("dp", None, None),
        P(),
        P("expert", None, "dp"),
        P("expert", "dp", None),
    )
    return jax.shard_map(
        functools.partial(shards, mesh.shape["expert"], mesh.shape["dp"]),
        mesh=mesh,
        in_specs=placed,
        out_specs=(
            P(("dp", "expert"), None),
            P("expert", None, "dp"),
            P("expert", "dp", None),
            P(),
        ),
        check_vma=False,
    )
```

```python
import functools

import jax
import jax.numpy as jnp
from jax import lax
from jax.experimental import pallas as pl
from jax.experimental.pallas import tpu as pltpu
from jax.sharding import PartitionSpec as P

MESH = pl.DeviceIdType.MESH
BF16 = jnp.bfloat16
F32 = jnp.float32
SLOT = 2
SEG = 16
LANES = 128


def nn(left, right):
    return lax.dot_general(left, right, (((1,), (0,)), ((), ())), preferred_element_type=F32)


def nt(left, right):
    return lax.dot_general(left, right, (((1,), (1,)), ((), ())), preferred_element_type=F32)


def tn(left, right):
    return lax.dot_general(left, right, (((0,), (0,)), ((), ())), preferred_element_type=F32)


def iota(shape, dim):
    return lax.broadcasted_iota(jnp.int32, shape, dim)


def one_hot(mask):
    return jnp.where(mask, 1.0, 0.0).astype(BF16)


def split3(values):
    high = values.astype(BF16).astype(F32)
    rest = values - high
    mid = rest.astype(BF16).astype(F32)
    return high, mid, rest - mid


def normal_cdf(values):
    return 0.5 * (1.0 + lax.erf(values * 0.7071067811865476))


def exchange(axis, count, me, source, target, send_sem, recv_sem):
    copies = []
    for step in range(1, count):
        peer = lax.rem(me + step, count)
        copy = pltpu.make_async_remote_copy(
            src_ref=source(peer),
            dst_ref=target,
            send_sem=send_sem.at[step],
            recv_sem=recv_sem.at[step],
            device_id={axis: peer},
            device_id_type=MESH,
        )
        copy.start()
        copies.append(copy)
    return copies


def arrive(copies):
    for copy in copies:
        copy.wait_recv()


def route_kernel(
    experts, groups, tok_hbm, cot_hbm, cnt_hbm, pick_hbm, router_hbm, win_hbm, wout_hbm,
    x_hbm, og_hbm, act_hbm, pg_hbm, gt_hbm, gr_hbm,
    x_ref, og_ref, gt_ref, gr_ref, tok_ref, cot_ref, cnt_ref, pick_ref, router_ref, win, wout,
    send, recv, pack, act_ref, pg_ref, acc, rows_s, rows_r, ret_s, ret_r,
    term_s, term_r, sum_r, fin_r,
    in_sem, out_sem, d_ss, d_rs, p_ss, p_rs, r_ss, r_rs, b_ss, b_rs, t_ss, t_rs, s_ss, s_rs, f_ss, f_rs,
):
    me = lax.axis_index("expert")
    my_group = lax.axis_index("dp")
    toks, width = tok_ref.shape
    capacity = pick_ref.shape[1]
    hidden = win.shape[1]
    count = groups * capacity
    piece = send.shape[2]
    half = rows_s.shape[2]
    back = ret_s.shape[2]
    chunk = term_s.shape[2]

    barrier = pltpu.get_barrier_semaphore()
    for step in range(1, experts):
        pl.semaphore_signal(
            barrier, inc=1, device_id={"expert": lax.rem(me + step, experts)}, device_id_type=MESH
        )
    for step in range(1, groups):
        pl.semaphore_signal(
            barrier, inc=1, device_id={"dp": lax.rem(my_group + step, groups)}, device_id_type=MESH
        )
    loads = []
    for source, target in (
        (pick_hbm, pick_ref), (tok_hbm, tok_ref), (router_hbm, router_ref), (cnt_hbm, cnt_ref),
        (cot_hbm, cot_ref), (win_hbm, win), (wout_hbm, wout),
    ):
        loads.append(pltpu.make_async_copy(source, target, in_sem.at[len(loads)]))
    stores = []
    for source, target in (
        (x_ref, x_hbm), (og_ref, og_hbm), (act_ref, act_hbm), (pg_ref, pg_hbm), (gt_ref, gt_hbm), (gr_ref, gr_hbm)
    ):
        stores.append(pltpu.make_async_copy(source, target, out_sem.at[len(stores)]))
    load_pick, load_tok, load_router, load_cnt, load_cot, load_in, load_out = loads
    for load in loads[:5]:
        load.start()

    load_pick.wait()
    picks = pick_ref[...]
    owner = picks // toks
    place = picks - owner * toks
    codes = jnp.concatenate([owner, place], axis=1).astype(F32).astype(BF16)
    wide = experts * SEG
    spread = one_hot(iota((wide, experts), 0) // SEG == iota((wide, experts), 1))
    spread_codes = nn(spread, codes)
    held = spread_codes[:, :capacity] == me.astype(F32)
    spots = spread_codes[:, capacity:]
    first = jnp.min(jnp.where(held, spots, 1e6), axis=1, keepdims=True)
    last = jnp.max(jnp.where(held, spots, -1.0), axis=1, keepdims=True)
    last = jnp.where(last > first, last, -1.0)
    seat = iota((wide, toks), 0) % SEG
    token_id = iota((wide, toks), 1).astype(F32)
    hit = (token_id == jnp.where(seat % SLOT == 0, first, last)).astype(F32)
    late = seat % (2 * SLOT) >= SLOT
    take = jnp.concatenate([jnp.where(late, 0.0, hit), jnp.where(late, hit, 0.0)], axis=1)
    part_of = iota((wide, 2 * toks), 0) % SEG // (2 * SLOT)

    load_tok.wait()
    load_router.wait()
    tok = tok_ref[...]
    router = router_ref[...]
    stacked = jnp.concatenate(split3(router), axis=0).astype(BF16)
    parts = nt(stacked, tok)
    load_cnt.wait()
    load_cot.wait()
    load_in.start()
    load_out.start()
    weight_row = jnp.maximum(cnt_ref[...], 1).astype(F32)
    diagonal = iota((toks, toks), 0) == iota((toks, toks), 1)
    weight = jnp.sum(jnp.where(diagonal, weight_row, 0.0), axis=1, keepdims=True)
    scaled = (cot_ref[...].astype(F32) / weight).astype(BF16)
    logits = parts[:experts] + parts[experts : 2 * experts] + parts[2 * experts :]
    raised = jnp.exp(logits - jnp.max(logits, axis=0, keepdims=True))
    prob = raised / jnp.sum(raised, axis=0, keepdims=True)

    pieces = SEG // (2 * SLOT)
    both = jnp.concatenate([tok, scaled], axis=0)
    total = jnp.zeros((wide, piece), F32)
    for part in range(pieces):
        low = part * piece
        high = min(width, low + piece)
        chosen = jnp.where(part_of == part, take, 0.0).astype(BF16)
        term = nn(chosen, both[:, low:high])
        if part == pieces - 1:
            padded = jnp.concatenate(
                split3(prob) + (jnp.zeros((LANES - 3 * experts, toks), F32),), axis=0
            )
            columns = [term, nt(chosen[:, toks:], padded.astype(BF16))]
            spare = piece - (high - low) - LANES
            if spare:
                columns.append(jnp.zeros((wide, spare), F32))
            term = jnp.concatenate(columns, axis=1)
        total = total + term
    send[...] = total.astype(BF16).reshape(experts, SEG, piece)
    recv[pl.ds(me, 1)] = send[pl.ds(me, 1)]

    pl.semaphore_wait(barrier, experts - 1 + groups - 1)
    dispatch = exchange("expert", experts, me, lambda peer: send.at[peer], recv.at[me], d_ss, d_rs)

    mine = iota((experts, capacity), 0) == me
    owner_row = jnp.sum(jnp.where(mine, owner, 0), axis=0, keepdims=True)
    tall = 2 * capacity
    slot_row = iota((tall, capacity), 0) % capacity
    slot_col = iota((tall, capacity), 1)
    owner_col = jnp.sum(jnp.where(slot_row == slot_col, owner_row, 0), axis=1, keepdims=True)
    same = owner_col == owner_row
    rank_col = jnp.sum(jnp.where(same & (slot_col < slot_row), 1, 0), axis=1, keepdims=True)
    seat_c = iota((tall, wide), 1) % SEG
    is_dy = jnp.where(iota((tall, wide), 0) >= capacity, 1, 0)
    wanted = (iota((tall, wide), 1) // SEG == owner_col) & (
        seat_c % (2 * SLOT) == SLOT * is_dy + rank_col
    )
    blocks = [one_hot(wanted & (seat_c // (2 * SLOT) == part)) for part in range(pieces)]
    before = same[:capacity] & (slot_row[:capacity] < slot_col[:capacity])
    rank_row = jnp.sum(jnp.where(before, 1, 0), axis=0, keepdims=True)
    row_u = iota((wide, capacity), 0)
    from_owner = row_u // SEG == owner_row
    hit_turned = hit.T
    seat_turned = iota((toks, wide), 1) % SEG

    arrive(dispatch)
    rows_in = recv[...].reshape(wide, piece)
    whole = pack.shape[2]
    for part in range(pieces):
        low = part * piece
        high = min(whole, low + piece)
        packed = nn(blocks[part], rows_in[:, : high - low]).astype(BF16)
        pack[pl.ds(my_group, 1), :, low:high] = packed[None]
    gather = exchange("dp", groups, my_group, lambda peer: pack.at[my_group], pack.at[my_group], p_ss, p_rs)
    load_in.wait()
    load_out.wait()
    arrive(gather)

    every = pack[...].astype(F32)
    x_rows = every[:, :capacity, :width].reshape(count, width).astype(BF16)
    dy_wide = every[:, capacity:, :width].reshape(count, width)
    gate_lanes = every[:, capacity:, width : width + LANES].reshape(count, LANES)
    lane = iota((count, LANES), 1)
    gate = jnp.sum(jnp.where(lane == me, gate_lanes, 0.0), axis=1, keepdims=True)
    dy_rows = dy_wide.astype(BF16)
    x_ref[...] = x_rows
    og_ref[...] = (gate * dy_wide).astype(BF16)
    stores[0].start()
    stores[1].start()

    step_cols = min(hidden, 256)
    gate_part = jnp.zeros((count, 1), F32)
    for tile in range(hidden // step_cols):
        cols = slice(tile * step_cols, (tile + 1) * step_cols)
        pre = nn(x_rows, win[:, cols])
        back_act = nt(dy_rows, wout[cols, :])
        cdf = normal_cdf(pre)
        act = (pre * cdf).astype(BF16)
        slope = cdf + pre * jnp.exp(-0.5 * pre * pre) * 0.3989422804014327
        act_ref[:, cols] = act
        pg_ref[:, cols] = (gate * back_act * slope).astype(BF16)
        gate_part = gate_part + jnp.sum(act.astype(F32) * back_act, axis=1, keepdims=True)

    stores[2].start()
    stores[3].start()

    fold_row, fold_col = iota((LANES, LANES), 0), iota((LANES, LANES), 1)
    fold = one_hot((fold_row % experts == fold_col) & (fold_row < 3 * experts))
    row_prob = nn(gate_lanes.astype(BF16), fold)
    own_prob = jnp.sum(jnp.where(lane == me, row_prob, 0.0), axis=1, keepdims=True)
    logit_part = gate_part * row_prob * (jnp.where(lane == me, 1.0, 0.0) - own_prob)
    term = tn(
        jnp.concatenate(split3(logit_part), axis=0).astype(BF16),
        jnp.concatenate([x_rows, x_rows, x_rows], axis=0),
    )[:experts]
    for part in range(experts):
        low = part * chunk
        high = min(width, low + chunk)
        if high <= low:
            term_s[part] = jnp.zeros((experts, chunk), F32)
            continue
        value = term[:, low:high]
        if high - low < chunk:
            value = jnp.concatenate([value, jnp.zeros((experts, chunk - high + low), F32)], axis=1)
        term_s[part] = value
    term_r[pl.ds(me, 1)] = term_s[pl.ds(me, 1)]
    scatter = exchange("expert", experts, me, lambda peer: term_s.at[peer], term_r.at[me], t_ss, t_rs)

    for tile in range(hidden // step_cols):
        cols = slice(tile * step_cols, (tile + 1) * step_cols)
        term = nt(pg_ref[:, cols], win[:, cols])
        if tile == 0:
            acc[...] = term
        else:
            acc[...] += term
    row_part = acc[...].reshape(groups, capacity, width)
    g1, g2, g3 = split3(gate_part)
    gate_tile = jnp.where(lane == 0, g1, jnp.where(lane == 1, g2, jnp.where(lane == 2, g3, 0.0)))
    right = [row_part[:, :, half:], gate_tile.reshape(groups, capacity, LANES)]
    if 2 * half > width + LANES:
        right.append(jnp.zeros((groups, capacity, 2 * half - width - LANES), F32))
    rows_s[...] = jnp.concatenate(
        [row_part[:, :, :half], jnp.concatenate(right, axis=2)], axis=1
    ).astype(BF16)
    rows_r[pl.ds(my_group, 1)] = rows_s[pl.ds(my_group, 1)]
    row_sum = exchange("dp", groups, my_group, lambda peer: rows_s.at[peer], rows_r.at[my_group], r_ss, r_rs)

    arrive(scatter)
    term_sum = term_r[0]
    for part in range(1, experts):
        term_sum = term_sum + term_r[part]
    sum_r[pl.ds(my_group, 1)] = term_sum[None]
    over_dp = exchange("dp", groups, my_group, lambda peer: sum_r.at[my_group], sum_r.at[my_group], s_ss, s_rs)

    arrive(row_sum)
    row_total = rows_r[0].astype(F32)
    for group in range(1, groups):
        row_total = row_total + rows_r[group].astype(F32)
    rest = width - half
    gate_lanes = row_total[capacity:, rest : rest + LANES]
    gate_total = jnp.sum(gate_lanes, axis=1, keepdims=True)
    row_grad = jnp.concatenate(
        [
            row_total[:capacity],
            row_total[capacity:, :rest],
            jnp.where(iota((capacity, LANES), 1) == me, gate_total, 0.0),
        ],
        axis=1,
    ).astype(BF16).astype(F32)
    returned = jnp.zeros((wide, back), F32)
    back_pieces = -(-(width + LANES) // back)
    for part in range(back_pieces):
        low = part * back
        high = min(width + LANES, low + back)
        give = jnp.where(from_owner & (row_u % SEG == SLOT * part + rank_row), 1.0, 0.0)
        term = nn(give, row_grad[:, low:high])
        if high - low < back:
            term = jnp.concatenate([term, jnp.zeros((wide, back - high + low), F32)], axis=1)
        returned = returned + term
    ret_s[...] = returned.astype(BF16).reshape(experts, SEG, back)
    ret_r[pl.ds(me, 1)] = ret_s[pl.ds(me, 1)]
    give_back = exchange("expert", experts, me, lambda peer: ret_s.at[peer], ret_r.at[me], b_ss, b_rs)

    arrive(over_dp)
    final = sum_r[0]
    for group in range(1, groups):
        final = final + sum_r[group]
    fin_r[pl.ds(me, 1)] = final[None]
    spread_out = exchange("expert", experts, me, lambda peer: fin_r.at[me], fin_r.at[me], f_ss, f_rs)

    marks = [
        jnp.where(seat_turned // SLOT == part, hit_turned, 0.0).astype(BF16)
        for part in range(back_pieces)
    ]
    r1, r2, r3 = split3(router)
    near = jnp.concatenate([r1, r2, r1, r3, r1, r2], axis=0).astype(BF16)

    arrive(give_back)
    ret_rows = ret_r[...].reshape(wide, back)
    gate_low = width - (back_pieces - 1) * back
    prob_grad = nt(
        ret_rows[:, gate_low : gate_low + LANES].T, marks[back_pieces - 1]
    )[:experts]
    logit_grad = prob * (prob_grad - jnp.sum(prob * prob_grad, axis=0, keepdims=True))
    l1, l2, l3 = split3(logit_grad)
    left = jnp.concatenate([l1, l1, l2, l1, l3, l2], axis=0).astype(BF16)
    gt_wide = tn(left, near)
    for part in range(back_pieces):
        low = part * back
        high = min(width, low + back)
        expert_sum = nn(marks[part], ret_rows[:, : high - low])
        gt_ref[:, low:high] = (expert_sum + gt_wide[:, low:high]).astype(BF16)

    stores[4].start()

    arrive(spread_out)
    for part in range(experts):
        low = part * chunk
        high = min(width, low + chunk)
        if high > low:
            gr_ref[:, low:high] = fin_r[part][:, : high - low]
    stores[5].start()
    for store in stores:
        store.wait()
    for copies in (dispatch, gather, row_sum, give_back, scatter, over_dp, spread_out):
        for copy in copies:
            copy.wait_send()


def weight_kernel(
    x_hbm, og_hbm, act_hbm, pg_hbm, gt_in, gr_in, gt_hbm, gin_hbm, gout_hbm, gr_hbm,
    x_ref, og_ref, act_ref, pg_ref, gin_ref, gout_ref, in_sem, out_sem,
):
    loads = []
    for source, target in (
        (x_hbm, x_ref), (pg_hbm, pg_ref), (act_hbm, act_ref), (og_hbm, og_ref), (gt_in, gt_hbm), (gr_in, gr_hbm)
    ):
        loads.append(pltpu.make_async_copy(source, target, in_sem.at[len(loads)]))
        loads[-1].start()
    stores = []

    def product(left, right, held, target):
        rows = held.shape[0]
        for low in range(0, rows, 256):
            span = slice(low, min(rows, low + 256))
            held[span, :] = tn(left[:, span], right[...]).astype(BF16)
            stores.append(pltpu.make_async_copy(held.at[span], target.at[0, span], out_sem.at[len(stores)]))
            stores[-1].start()

    loads[0].wait()
    loads[1].wait()
    product(x_ref, pg_ref, gin_ref, gin_hbm)
    loads[2].wait()
    loads[3].wait()
    product(act_ref, og_ref, gout_ref, gout_hbm)
    for copy in loads[4:] + stores:
        copy.wait()


def shards(experts, groups, tokens, cotangent, counts, picks, router, w_in, w_out):
    toks, width = tokens.shape
    capacity = picks.shape[2]
    hidden = w_in.shape[2]
    count = groups * capacity
    tiles = -(-width // LANES)
    pieces = SEG // (2 * SLOT)
    piece = LANES * -(-(tiles + 1) // pieces)
    whole = width + LANES
    half = LANES * -(-(tiles + 1) // 2)
    back = LANES * -(-(tiles + 1) // (SEG // SLOT))
    chunk = LANES * -(-tiles // experts)
    hbm = pl.BlockSpec(memory_space=pltpu.HBM)
    dma = pltpu.SemaphoreType.DMA
    over_e, over_g = dma((experts,)), dma((groups,))
    row_scratch = [
        pltpu.VMEM((count, width), BF16),
        pltpu.VMEM((count, width), BF16),
    ]
    results = pl.pallas_call(
        functools.partial(route_kernel, experts, groups),
        out_shape=(
            jax.ShapeDtypeStruct((count, width), BF16),
            jax.ShapeDtypeStruct((count, width), BF16),
            jax.ShapeDtypeStruct((count, hidden), BF16),
            jax.ShapeDtypeStruct((count, hidden), BF16),
            jax.ShapeDtypeStruct((toks, width), BF16),
            jax.ShapeDtypeStruct((experts, width), F32),
        ),
        in_specs=[hbm] * 7,
        out_specs=(hbm,) * 6,
        scratch_shapes=row_scratch
        + [
            pltpu.VMEM((toks, width), BF16),
            pltpu.VMEM((experts, width), F32),
            pltpu.VMEM((toks, width), BF16),
            pltpu.VMEM((toks, width), BF16),
            pltpu.VMEM((1, toks), jnp.int32),
            pltpu.VMEM((experts, capacity), jnp.int32),
            pltpu.VMEM((experts, width), F32),
            pltpu.VMEM((width, hidden), BF16),
            pltpu.VMEM((hidden, width), BF16),
            pltpu.VMEM((experts, SEG, piece), BF16),
            pltpu.VMEM((experts, SEG, piece), BF16),
            pltpu.VMEM((groups, 2 * capacity, whole), BF16),
            pltpu.VMEM((count, hidden), BF16),
            pltpu.VMEM((count, hidden), BF16),
            pltpu.VMEM((count, width), F32),
            pltpu.VMEM((groups, 2 * capacity, half), BF16),
            pltpu.VMEM((groups, 2 * capacity, half), BF16),
            pltpu.VMEM((experts, SEG, back), BF16),
            pltpu.VMEM((experts, SEG, back), BF16),
            pltpu.VMEM((experts, experts, chunk), F32),
            pltpu.VMEM((experts, experts, chunk), F32),
            pltpu.VMEM((groups, experts, chunk), F32),
            pltpu.VMEM((experts, experts, chunk), F32),
            dma((7,)),
            dma((6,)),
            over_e, over_e,
            over_g, over_g,
            over_g, over_g,
            over_e, over_e,
            over_e, over_e,
            over_g, over_g,
            over_e, over_e,
        ],
        compiler_params=pltpu.CompilerParams(
            collective_id=0, has_side_effects=True, vmem_limit_bytes=58 * 1024 * 1024
        ),
        name="route",
    )(tokens, cotangent, counts.reshape(1, toks), picks[0], router.T, w_in[0], w_out[0])

    grad_tokens, grad_in, grad_out, grad_router = pl.pallas_call(
        weight_kernel,
        out_shape=(
            jax.ShapeDtypeStruct((toks, width), BF16),
            jax.ShapeDtypeStruct((1, width, hidden), BF16),
            jax.ShapeDtypeStruct((1, hidden, width), BF16),
            jax.ShapeDtypeStruct((experts, width), F32),
        ),
        in_specs=[hbm] * 6,
        out_specs=(hbm,) * 4,
        scratch_shapes=row_scratch
        + [
            pltpu.VMEM((count, hidden), BF16),
            pltpu.VMEM((count, hidden), BF16),
            pltpu.VMEM((width, hidden), BF16),
            pltpu.VMEM((hidden, width), BF16),
            dma((6,)),
            dma((-(-width // 256) + -(-hidden // 256),)),
        ],
        compiler_params=pltpu.CompilerParams(vmem_limit_bytes=58 * 1024 * 1024),
        name="weight_grads",
    )(*results)
    return grad_tokens, grad_in, grad_out, grad_router.T


def solution(mesh):
    placed = (
        P(("dp", "expert"), None),
        P(("dp", "expert"), None),
        P(("dp", "expert")),
        P("dp", None, None),
        P(),
        P("expert", None, "dp"),
        P("expert", "dp", None),
    )
    return jax.shard_map(
        functools.partial(shards, mesh.shape["expert"], mesh.shape["dp"]),
        mesh=mesh,
        in_specs=placed,
        out_specs=(
            P(("dp", "expert"), None),
            P("expert", None, "dp"),
            P("expert", "dp", None),
            P(),
        ),
        check_vma=False,
    )
```

```python
import functools

import jax
import jax.numpy as jnp
from jax import lax
from jax.experimental import pallas as pl
from jax.experimental.pallas import tpu as pltpu
from jax.sharding import PartitionSpec as P

MESH = pl.DeviceIdType.MESH
BF16 = jnp.bfloat16
F32 = jnp.float32
SLOT = 2
SEG = 16
LANES = 128


def nn(left, right):
    return lax.dot_general(left, right, (((1,), (0,)), ((), ())), preferred_element_type=F32)


def nt(left, right):
    return lax.dot_general(left, right, (((1,), (1,)), ((), ())), preferred_element_type=F32)


def tn(left, right):
    return lax.dot_general(left, right, (((0,), (0,)), ((), ())), preferred_element_type=F32)


def iota(shape, dim):
    return lax.broadcasted_iota(jnp.int32, shape, dim)


def one_hot(mask):
    return jnp.where(mask, 1.0, 0.0).astype(BF16)


def split3(values):
    high = values.astype(BF16).astype(F32)
    rest = values - high
    mid = rest.astype(BF16).astype(F32)
    return high, mid, rest - mid


def normal_cdf(values):
    return 0.5 * (1.0 + lax.erf(values * 0.7071067811865476))


def exchange(axis, count, me, source, target, send_sem, recv_sem):
    copies = []
    for step in range(1, count):
        peer = lax.rem(me + step, count)
        copy = pltpu.make_async_remote_copy(
            src_ref=source(peer),
            dst_ref=target,
            send_sem=send_sem.at[step],
            recv_sem=recv_sem.at[step],
            device_id={axis: peer},
            device_id_type=MESH,
        )
        copy.start()
        copies.append(copy)
    return copies


def arrive(copies):
    for copy in copies:
        copy.wait_recv()


def route_kernel(
    experts, groups, tok_hbm, cot_hbm, cnt_hbm, pick_hbm, router_hbm, win_hbm, wout_hbm,
    x_hbm, og_hbm, act_hbm, pg_hbm, gt_hbm, gr_hbm,
    x_ref, og_ref, gt_ref, gr_ref, tok_ref, cot_ref, cnt_ref, pick_ref, router_ref, win, wout,
    send, recv, pack_x, pack_d, act_ref, pg_ref, slope_ref, head_s, head_r, tail_s, tail_r, ret_s, ret_r,
    term_s, term_r, sum_r, fin_r,
    in_sem, out_sem, d_ss, d_rs, x_ss, x_rs, y_ss, y_rs, h_ss, h_rs, r_ss, r_rs, b_ss, b_rs, t_ss, t_rs, s_ss, s_rs, f_ss, f_rs,
):
    me = lax.axis_index("expert")
    my_group = lax.axis_index("dp")
    toks, width = tok_ref.shape
    capacity = pick_ref.shape[1]
    hidden = win.shape[1]
    count = groups * capacity
    piece = send.shape[2]
    half = pack_x.shape[2]
    whole = 2 * half
    head = 2 * head_s.shape[2]
    back = ret_s.shape[2]
    chunk = term_s.shape[2]

    barrier = pltpu.get_barrier_semaphore()
    for step in range(1, experts):
        pl.semaphore_signal(
            barrier, inc=1, device_id={"expert": lax.rem(me + step, experts)}, device_id_type=MESH
        )
    for step in range(1, groups):
        pl.semaphore_signal(
            barrier, inc=1, device_id={"dp": lax.rem(my_group + step, groups)}, device_id_type=MESH
        )
    loads = []
    for source, target in (
        (pick_hbm, pick_ref), (tok_hbm, tok_ref), (router_hbm, router_ref), (cnt_hbm, cnt_ref),
        (cot_hbm, cot_ref), (win_hbm, win), (wout_hbm, wout),
    ):
        loads.append(pltpu.make_async_copy(source, target, in_sem.at[len(loads)]))
    stores = []
    for source, target in (
        (x_ref, x_hbm), (og_ref, og_hbm), (act_ref, act_hbm), (pg_ref, pg_hbm), (gt_ref, gt_hbm), (gr_ref, gr_hbm)
    ):
        stores.append(pltpu.make_async_copy(source, target, out_sem.at[len(stores)]))
    load_pick, load_tok, load_router, load_cnt, load_cot, load_in, load_out = loads
    for load in loads[:5]:
        load.start()

    load_pick.wait()
    picks = pick_ref[...]
    owner = picks // toks
    place = picks - owner * toks
    codes = jnp.concatenate([owner, place], axis=1).astype(F32).astype(BF16)
    wide = experts * SEG
    spread = one_hot(iota((wide, experts), 0) // SEG == iota((wide, experts), 1))
    spread_codes = nn(spread, codes)
    held = spread_codes[:, :capacity] == me.astype(F32)
    spots = spread_codes[:, capacity:]
    first = jnp.min(jnp.where(held, spots, 1e6), axis=1, keepdims=True)
    last = jnp.max(jnp.where(held, spots, -1.0), axis=1, keepdims=True)
    last = jnp.where(last > first, last, -1.0)
    seat = iota((wide, toks), 0) % SEG
    token_id = iota((wide, toks), 1).astype(F32)
    hit = (token_id == jnp.where(seat % SLOT == 0, first, last)).astype(F32)
    late = seat % (2 * SLOT) >= SLOT
    take = jnp.concatenate([jnp.where(late, 0.0, hit), jnp.where(late, hit, 0.0)], axis=1)
    part_of = iota((wide, 2 * toks), 0) % SEG // (2 * SLOT)

    load_tok.wait()
    load_router.wait()
    tok = tok_ref[...]
    router = router_ref[...]
    stacked = jnp.concatenate(split3(router), axis=0).astype(BF16)
    parts = nt(stacked, tok)
    load_cnt.wait()
    load_cot.wait()
    load_in.start()
    load_out.start()
    weight_row = jnp.maximum(cnt_ref[...], 1).astype(F32)
    diagonal = iota((toks, toks), 0) == iota((toks, toks), 1)
    weight = jnp.sum(jnp.where(diagonal, weight_row, 0.0), axis=1, keepdims=True)
    scaled = (cot_ref[...].astype(F32) / weight).astype(BF16)
    logits = parts[:experts] + parts[experts : 2 * experts] + parts[2 * experts :]
    raised = jnp.exp(logits - jnp.max(logits, axis=0, keepdims=True))
    prob = raised / jnp.sum(raised, axis=0, keepdims=True)

    pieces = SEG // (2 * SLOT)
    both = jnp.concatenate([tok, scaled], axis=0)
    total = jnp.zeros((wide, piece), F32)
    for part in range(pieces):
        low = part * piece
        high = min(width, low + piece)
        chosen = jnp.where(part_of == part, take, 0.0).astype(BF16)
        term = nn(chosen, both[:, low:high])
        if part == pieces - 1:
            padded = jnp.concatenate(
                split3(prob) + (jnp.zeros((LANES - 3 * experts, toks), F32),), axis=0
            )
            columns = [term, nt(chosen[:, toks:], padded.astype(BF16))]
            spare = piece - (high - low) - LANES
            if spare:
                columns.append(jnp.zeros((wide, spare), F32))
            term = jnp.concatenate(columns, axis=1)
        total = total + term
    send[...] = total.astype(BF16).reshape(experts, SEG, piece)
    recv[pl.ds(me, 1)] = send[pl.ds(me, 1)]

    pl.semaphore_wait(barrier, experts - 1 + groups - 1)
    dispatch = exchange("expert", experts, me, lambda peer: send.at[peer], recv.at[me], d_ss, d_rs)

    mine = iota((experts, capacity), 0) == me
    owner_row = jnp.sum(jnp.where(mine, owner, 0), axis=0, keepdims=True)
    tall = 2 * capacity
    slot_row = iota((tall, capacity), 0) % capacity
    slot_col = iota((tall, capacity), 1)
    owner_col = jnp.sum(jnp.where(slot_row == slot_col, owner_row, 0), axis=1, keepdims=True)
    same = owner_col == owner_row
    rank_col = jnp.sum(jnp.where(same & (slot_col < slot_row), 1, 0), axis=1, keepdims=True)
    seat_c = iota((tall, wide), 1) % SEG
    is_dy = jnp.where(iota((tall, wide), 0) >= capacity, 1, 0)
    wanted = (iota((tall, wide), 1) // SEG == owner_col) & (
        seat_c % (2 * SLOT) == SLOT * is_dy + rank_col
    )
    blocks = [one_hot(wanted & (seat_c // (2 * SLOT) == part)) for part in range(pieces)]
    before = same[:capacity] & (slot_row[:capacity] < slot_col[:capacity])
    rank_row = jnp.sum(jnp.where(before, 1, 0), axis=0, keepdims=True)
    row_u = iota((wide, capacity), 0)
    from_owner = row_u // SEG == owner_row
    hit_turned = hit.T
    seat_turned = iota((toks, wide), 1) % SEG

    arrive(dispatch)
    rows_in = recv[...].reshape(wide, piece)
    packed = []
    for part in range(pieces):
        taken = min(whole, (part + 1) * piece) - part * piece
        packed.append(nn(blocks[part], rows_in[:, :taken]))
    packed = jnp.concatenate(packed, axis=1)

    def folded(rows):
        return jnp.concatenate([rows[..., :half], rows[..., half:]], axis=-2).astype(BF16)

    def unfolded(pack):
        rows = pack[...].astype(F32)
        return jnp.concatenate([rows[:, :capacity], rows[:, capacity:]], axis=2).reshape(count, whole)

    pack_x[pl.ds(my_group, 1)] = folded(packed[:capacity])[None]
    gather_x = exchange(
        "dp", groups, my_group, lambda peer: pack_x.at[my_group], pack_x.at[my_group], x_ss, x_rs
    )
    pack_d[pl.ds(my_group, 1)] = folded(packed[capacity:])[None]
    gather_d = exchange(
        "dp", groups, my_group, lambda peer: pack_d.at[my_group], pack_d.at[my_group], y_ss, y_rs
    )
    load_in.wait()
    load_out.wait()
    arrive(gather_x)

    x_rows = unfolded(pack_x)[:, :width].astype(BF16)
    x_ref[...] = x_rows
    stores[0].start()
    step_cols = min(hidden, 256)
    for tile in range(hidden // step_cols):
        cols = slice(tile * step_cols, (tile + 1) * step_cols)
        pre = nn(x_rows, win[:, cols])
        cdf = normal_cdf(pre)
        act_ref[:, cols] = (pre * cdf).astype(BF16)
        slope_ref[:, cols] = cdf + pre * jnp.exp(-0.5 * pre * pre) * 0.3989422804014327
    stores[2].start()

    arrive(gather_d)
    dy_full = unfolded(pack_d)
    dy_wide = dy_full[:, :width]
    gate_lanes = dy_full[:, width : width + LANES]
    lane = iota((count, LANES), 1)
    gate = jnp.sum(jnp.where(lane == me, gate_lanes, 0.0), axis=1, keepdims=True)
    dy_rows = dy_wide.astype(BF16)
    gate_part = jnp.zeros((count, 1), F32)
    for tile in range(hidden // step_cols):
        cols = slice(tile * step_cols, (tile + 1) * step_cols)
        back_act = nt(dy_rows, wout[cols, :])
        pg_ref[:, cols] = (gate * back_act * slope_ref[:, cols]).astype(BF16)
        gate_part = gate_part + jnp.sum(act_ref[:, cols].astype(F32) * back_act, axis=1, keepdims=True)
    stores[3].start()
    og_ref[...] = (gate * dy_wide).astype(BF16)
    stores[1].start()

    fold_row, fold_col = iota((LANES, LANES), 0), iota((LANES, LANES), 1)
    fold = one_hot((fold_row % experts == fold_col) & (fold_row < 3 * experts))
    row_prob = nn(gate_lanes.astype(BF16), fold)
    own_prob = jnp.sum(jnp.where(lane == me, row_prob, 0.0), axis=1, keepdims=True)
    logit_part = gate_part * row_prob * (jnp.where(lane == me, 1.0, 0.0) - own_prob)
    term = tn(
        jnp.concatenate(split3(logit_part), axis=0).astype(BF16),
        jnp.concatenate([x_rows, x_rows, x_rows], axis=0),
    )[:experts]
    for part in range(experts):
        low = part * chunk
        high = min(width, low + chunk)
        if high <= low:
            term_s[part] = jnp.zeros((experts, chunk), F32)
            continue
        value = term[:, low:high]
        if high - low < chunk:
            value = jnp.concatenate([value, jnp.zeros((experts, chunk - high + low), F32)], axis=1)
        term_s[part] = value
    term_r[pl.ds(me, 1)] = term_s[pl.ds(me, 1)]
    scatter = exchange("expert", experts, me, lambda peer: term_s.at[peer], term_r.at[me], t_ss, t_rs)

    pre_grad = pg_ref[...]

    def row_columns(low, high):
        return [
            nt(pre_grad, win[start : min(high, start + 256), :]) for start in range(low, high, 256)
        ]

    def to_groups(columns, sent, kept, send_sem, recv_sem):
        rows = jnp.concatenate(columns, axis=1).reshape(groups, capacity, 2 * sent.shape[2])
        side = sent.shape[2]
        sent[...] = jnp.concatenate([rows[:, :, :side], rows[:, :, side:]], axis=1).astype(BF16)
        kept[pl.ds(my_group, 1)] = sent[pl.ds(my_group, 1)]
        return exchange(
            "dp", groups, my_group, lambda peer: sent.at[peer], kept.at[my_group], send_sem, recv_sem
        )

    head_sum = to_groups(row_columns(0, head), head_s, head_r, h_ss, h_rs)
    g1, g2, g3 = split3(gate_part)
    tail = row_columns(head, width)
    tail.append(jnp.where(lane == 0, g1, jnp.where(lane == 1, g2, jnp.where(lane == 2, g3, 0.0))))
    spare = head + 2 * tail_s.shape[2] - width - LANES
    if spare:
        tail.append(jnp.zeros((count, spare), F32))
    tail_sum = to_groups(tail, tail_s, tail_r, r_ss, r_rs)

    arrive(scatter)
    term_sum = term_r[0]
    for part in range(1, experts):
        term_sum = term_sum + term_r[part]
    sum_r[pl.ds(my_group, 1)] = term_sum[None]
    over_dp = exchange("dp", groups, my_group, lambda peer: sum_r.at[my_group], sum_r.at[my_group], s_ss, s_rs)

    def over_blocks(kept):
        summed = kept[0].astype(F32)
        for group in range(1, groups):
            summed = summed + kept[group].astype(F32)
        return [summed[:capacity], summed[capacity:]]

    arrive(head_sum)
    row_sides = over_blocks(head_r)
    arrive(tail_sum)
    row_total = jnp.concatenate(row_sides + over_blocks(tail_r), axis=1)
    gate_total = jnp.sum(row_total[:, width : width + LANES], axis=1, keepdims=True)
    row_grad = jnp.concatenate(
        [
            row_total[:, :width],
            jnp.where(iota((capacity, LANES), 1) == me, gate_total, 0.0),
        ],
        axis=1,
    ).astype(BF16).astype(F32)
    returned = jnp.zeros((wide, back), F32)
    back_pieces = -(-(width + LANES) // back)
    for part in range(back_pieces):
        low = part * back
        high = min(width + LANES, low + back)
        give = jnp.where(from_owner & (row_u % SEG == SLOT * part + rank_row), 1.0, 0.0)
        term = nn(give, row_grad[:, low:high])
        if high - low < back:
            term = jnp.concatenate([term, jnp.zeros((wide, back - high + low), F32)], axis=1)
        returned = returned + term
    ret_s[...] = returned.astype(BF16).reshape(experts, SEG, back)
    ret_r[pl.ds(me, 1)] = ret_s[pl.ds(me, 1)]
    give_back = exchange("expert", experts, me, lambda peer: ret_s.at[peer], ret_r.at[me], b_ss, b_rs)

    arrive(over_dp)
    final = sum_r[0]
    for group in range(1, groups):
        final = final + sum_r[group]
    fin_r[pl.ds(me, 1)] = final[None]
    spread_out = exchange("expert", experts, me, lambda peer: fin_r.at[me], fin_r.at[me], f_ss, f_rs)

    marks = [
        jnp.where(seat_turned // SLOT == part, hit_turned, 0.0).astype(BF16)
        for part in range(back_pieces)
    ]
    r1, r2, r3 = split3(router)
    near = jnp.concatenate([r1, r2, r1, r3, r1, r2], axis=0).astype(BF16)

    arrive(give_back)
    ret_rows = ret_r[...].reshape(wide, back)
    gate_low = width - (back_pieces - 1) * back
    prob_grad = nt(
        ret_rows[:, gate_low : gate_low + LANES].T, marks[back_pieces - 1]
    )[:experts]
    logit_grad = prob * (prob_grad - jnp.sum(prob * prob_grad, axis=0, keepdims=True))
    l1, l2, l3 = split3(logit_grad)
    left = jnp.concatenate([l1, l1, l2, l1, l3, l2], axis=0).astype(BF16)
    gt_wide = tn(left, near)
    for part in range(back_pieces):
        low = part * back
        high = min(width, low + back)
        expert_sum = nn(marks[part], ret_rows[:, : high - low])
        gt_ref[:, low:high] = (expert_sum + gt_wide[:, low:high]).astype(BF16)

    stores[4].start()

    arrive(spread_out)
    for part in range(experts):
        low = part * chunk
        high = min(width, low + chunk)
        if high > low:
            gr_ref[:, low:high] = fin_r[part][:, : high - low]
    stores[5].start()
    for store in stores:
        store.wait()
    for copies in (dispatch, gather_x, gather_d, head_sum, tail_sum, give_back, scatter, over_dp, spread_out):
        for copy in copies:
            copy.wait_send()


def weight_kernel(
    x_hbm, og_hbm, act_hbm, pg_hbm, gt_in, gr_in, gt_hbm, gin_hbm, gout_hbm, gr_hbm,
    x_ref, og_ref, act_ref, pg_ref, gt_ref, gr_ref, gin_ref, gout_ref, in_sem, out_sem,
):
    loads = []
    for source, target in (
        (x_hbm, x_ref), (pg_hbm, pg_ref), (act_hbm, act_ref), (og_hbm, og_ref), (gt_in, gt_ref), (gr_in, gr_ref)
    ):
        loads.append(pltpu.make_async_copy(source, target, in_sem.at[len(loads)]))
        loads[-1].start()
    stores = []

    def product(left, right, held, target):
        rows = held.shape[0]
        for low in range(0, rows, 256):
            span = slice(low, min(rows, low + 256))
            held[span, :] = tn(left[:, span], right[...]).astype(BF16)
            stores.append(pltpu.make_async_copy(held.at[span], target.at[0, span], out_sem.at[len(stores)]))
            stores[-1].start()

    loads[0].wait()
    loads[1].wait()
    product(x_ref, pg_ref, gin_ref, gin_hbm)
    for load, held, target in ((loads[4], gt_ref, gt_hbm), (loads[5], gr_ref, gr_hbm)):
        load.wait()
        stores.append(pltpu.make_async_copy(held, target, out_sem.at[len(stores)]))
        stores[-1].start()
    loads[2].wait()
    loads[3].wait()
    product(act_ref, og_ref, gout_ref, gout_hbm)
    for store in stores:
        store.wait()


def shards(experts, groups, tokens, cotangent, counts, picks, router, w_in, w_out):
    toks, width = tokens.shape
    capacity = picks.shape[2]
    hidden = w_in.shape[2]
    count = groups * capacity
    tiles = -(-width // LANES)
    pieces = SEG // (2 * SLOT)
    piece = LANES * -(-(tiles + 1) // pieces)
    half = LANES * -(-(tiles + 1) // 2)
    back = LANES * -(-(tiles + 1) // (SEG // SLOT))
    head = LANES * ((tiles + 1) * 2 // 7)
    tail = half - head
    chunk = LANES * -(-tiles // experts)
    hbm = pl.BlockSpec(memory_space=pltpu.HBM)
    dma = pltpu.SemaphoreType.DMA
    over_e, over_g = dma((experts,)), dma((groups,))
    row_scratch = [
        pltpu.VMEM((count, width), BF16),
        pltpu.VMEM((count, width), BF16),
    ]
    results = pl.pallas_call(
        functools.partial(route_kernel, experts, groups),
        out_shape=(
            jax.ShapeDtypeStruct((count, width), BF16),
            jax.ShapeDtypeStruct((count, width), BF16),
            jax.ShapeDtypeStruct((count, hidden), BF16),
            jax.ShapeDtypeStruct((count, hidden), BF16),
            jax.ShapeDtypeStruct((toks, width), BF16),
            jax.ShapeDtypeStruct((experts, width), F32),
        ),
        in_specs=[hbm] * 7,
        out_specs=(hbm,) * 6,
        scratch_shapes=row_scratch
        + [
            pltpu.VMEM((toks, width), BF16),
            pltpu.VMEM((experts, width), F32),
            pltpu.VMEM((toks, width), BF16),
            pltpu.VMEM((toks, width), BF16),
            pltpu.VMEM((1, toks), jnp.int32),
            pltpu.VMEM((experts, capacity), jnp.int32),
            pltpu.VMEM((experts, width), F32),
            pltpu.VMEM((width, hidden), BF16),
            pltpu.VMEM((hidden, width), BF16),
            pltpu.VMEM((experts, SEG, piece), BF16),
            pltpu.VMEM((experts, SEG, piece), BF16),
            pltpu.VMEM((groups, 2 * capacity, half), BF16),
            pltpu.VMEM((groups, 2 * capacity, half), BF16),
            pltpu.VMEM((count, hidden), BF16),
            pltpu.VMEM((count, hidden), BF16),
            pltpu.VMEM((count, hidden), F32),
            pltpu.VMEM((groups, 2 * capacity, head), BF16),
            pltpu.VMEM((groups, 2 * capacity, head), BF16),
            pltpu.VMEM((groups, 2 * capacity, tail), BF16),
            pltpu.VMEM((groups, 2 * capacity, tail), BF16),
            pltpu.VMEM((experts, SEG, back), BF16),
            pltpu.VMEM((experts, SEG, back), BF16),
            pltpu.VMEM((experts, experts, chunk), F32),
            pltpu.VMEM((experts, experts, chunk), F32),
            pltpu.VMEM((groups, experts, chunk), F32),
            pltpu.VMEM((experts, experts, chunk), F32),
            dma((7,)),
            dma((6,)),
            over_e, over_e,
            over_g, over_g,
            over_g, over_g,
            over_g, over_g,
            over_g, over_g,
            over_e, over_e,
            over_e, over_e,
            over_g, over_g,
            over_e, over_e,
        ],
        compiler_params=pltpu.CompilerParams(
            collective_id=0, has_side_effects=True, vmem_limit_bytes=58 * 1024 * 1024
        ),
        name="route",
    )(tokens, cotangent, counts.reshape(1, toks), picks[0], router.T, w_in[0], w_out[0])

    grad_tokens, grad_in, grad_out, grad_router = pl.pallas_call(
        weight_kernel,
        out_shape=(
            jax.ShapeDtypeStruct((toks, width), BF16),
            jax.ShapeDtypeStruct((1, width, hidden), BF16),
            jax.ShapeDtypeStruct((1, hidden, width), BF16),
            jax.ShapeDtypeStruct((experts, width), F32),
        ),
        in_specs=[hbm] * 6,
        out_specs=(hbm,) * 4,
        scratch_shapes=row_scratch
        + [
            pltpu.VMEM((count, hidden), BF16),
            pltpu.VMEM((count, hidden), BF16),
            pltpu.VMEM((toks, width), BF16),
            pltpu.VMEM((experts, width), F32),
            pltpu.VMEM((width, hidden), BF16),
            pltpu.VMEM((hidden, width), BF16),
            dma((6,)),
            dma((-(-width // 256) + -(-hidden // 256) + 2,)),
        ],
        compiler_params=pltpu.CompilerParams(vmem_limit_bytes=58 * 1024 * 1024),
        name="weight_grads",
    )(*results)
    return grad_tokens, grad_in, grad_out, grad_router.T


def solution(mesh):
    placed = (
        P(("dp", "expert"), None),
        P(("dp", "expert"), None),
        P(("dp", "expert")),
        P("dp", None, None),
        P(),
        P("expert", None, "dp"),
        P("expert", "dp", None),
    )
    return jax.shard_map(
        functools.partial(shards, mesh.shape["expert"], mesh.shape["dp"]),
        mesh=mesh,
        in_specs=placed,
        out_specs=(
            P(("dp", "expert"), None),
            P("expert", None, "dp"),
            P("expert", "dp", None),
            P(),
        ),
        check_vma=False,
    )
```

```python
import functools

import jax
import jax.numpy as jnp
from jax import lax
from jax.experimental import pallas as pl
from jax.experimental.pallas import tpu as pltpu
from jax.sharding import PartitionSpec as P

MESH = pl.DeviceIdType.MESH
BF16 = jnp.bfloat16
F32 = jnp.float32
SLOT = 2
SEG = 16
LANES = 128


def nn(left, right):
    return lax.dot_general(left, right, (((1,), (0,)), ((), ())), preferred_element_type=F32)


def nt(left, right):
    return lax.dot_general(left, right, (((1,), (1,)), ((), ())), preferred_element_type=F32)


def tn(left, right):
    return lax.dot_general(left, right, (((0,), (0,)), ((), ())), preferred_element_type=F32)


def iota(shape, dim):
    return lax.broadcasted_iota(jnp.int32, shape, dim)


def one_hot(mask):
    return jnp.where(mask, 1.0, 0.0).astype(BF16)


def split3(values):
    high = values.astype(BF16).astype(F32)
    rest = values - high
    mid = rest.astype(BF16).astype(F32)
    return high, mid, rest - mid


def normal_cdf(values):
    return 0.5 * (1.0 + lax.erf(values * 0.7071067811865476))


def exchange(axis, count, me, source, target, send_sem, recv_sem):
    copies = []
    for step in range(1, count):
        peer = lax.rem(me + step, count)
        copy = pltpu.make_async_remote_copy(
            src_ref=source(peer),
            dst_ref=target,
            send_sem=send_sem.at[step],
            recv_sem=recv_sem.at[step],
            device_id={axis: peer},
            device_id_type=MESH,
        )
        copy.start()
        copies.append(copy)
    return copies


def arrive(copies):
    for copy in copies:
        copy.wait_recv()


def route_kernel(
    experts, groups, tok_hbm, cot_hbm, cnt_hbm, pick_hbm, router_hbm, win_hbm, wout_hbm,
    x_hbm, og_hbm, act_hbm, pg_hbm, gt_hbm, gr_hbm,
    x_ref, og_ref, gt_ref, gr_ref, tok_ref, cot_ref, cnt_ref, pick_ref, router_ref, win, wout,
    send, recv, gate_s, gate_r, pack_x, pack_d, act_ref, pg_ref, slope_ref, head_s, head_r, tail_s, tail_r, ret_s, ret_r,
    term_s, term_r, sum_r, fin_r,
    in_sem, out_sem, d_ss, d_rs, g_ss, g_rs, x_ss, x_rs, y_ss, y_rs, h_ss, h_rs, r_ss, r_rs, b_ss, b_rs, t_ss, t_rs, s_ss, s_rs, f_ss, f_rs,
):
    me = lax.axis_index("expert")
    my_group = lax.axis_index("dp")
    toks, width = tok_ref.shape
    capacity = pick_ref.shape[1]
    hidden = win.shape[1]
    count = groups * capacity
    piece = send.shape[2]
    half = pack_x.shape[2]
    whole = 2 * half
    head = 2 * head_s.shape[2]
    back = ret_s.shape[2]
    chunk = term_s.shape[2]

    barrier = pltpu.get_barrier_semaphore()
    for step in range(1, experts):
        pl.semaphore_signal(
            barrier, inc=1, device_id={"expert": lax.rem(me + step, experts)}, device_id_type=MESH
        )
    for step in range(1, groups):
        pl.semaphore_signal(
            barrier, inc=1, device_id={"dp": lax.rem(my_group + step, groups)}, device_id_type=MESH
        )
    loads = []
    for source, target in (
        (pick_hbm, pick_ref), (tok_hbm, tok_ref), (router_hbm, router_ref), (cnt_hbm, cnt_ref),
        (cot_hbm, cot_ref), (win_hbm, win), (wout_hbm, wout),
    ):
        loads.append(pltpu.make_async_copy(source, target, in_sem.at[len(loads)]))
    stores = []
    for source, target in (
        (x_ref, x_hbm), (og_ref, og_hbm), (act_ref, act_hbm), (pg_ref, pg_hbm), (gt_ref, gt_hbm), (gr_ref, gr_hbm)
    ):
        stores.append(pltpu.make_async_copy(source, target, out_sem.at[len(stores)]))
    load_pick, load_tok, load_router, load_cnt, load_cot, load_in, load_out = loads
    for load in loads[:5]:
        load.start()

    load_pick.wait()
    picks = pick_ref[...]
    owner = picks // toks
    place = picks - owner * toks
    codes = jnp.concatenate([owner, place], axis=1).astype(F32).astype(BF16)
    wide = experts * SEG
    spread = one_hot(iota((wide, experts), 0) // SEG == iota((wide, experts), 1))
    spread_codes = nn(spread, codes)
    held = spread_codes[:, :capacity] == me.astype(F32)
    spots = spread_codes[:, capacity:]
    first = jnp.min(jnp.where(held, spots, 1e6), axis=1, keepdims=True)
    last = jnp.max(jnp.where(held, spots, -1.0), axis=1, keepdims=True)
    last = jnp.where(last > first, last, -1.0)
    seat = iota((wide, toks), 0) % SEG
    token_id = iota((wide, toks), 1).astype(F32)
    hit = (token_id == jnp.where(seat % SLOT == 0, first, last)).astype(F32)
    late = seat % (2 * SLOT) >= SLOT
    take = jnp.concatenate([jnp.where(late, 0.0, hit), jnp.where(late, hit, 0.0)], axis=1)
    part_of = iota((wide, 2 * toks), 0) % SEG // (2 * SLOT)

    load_tok.wait()
    tok = tok_ref[...]
    load_cnt.wait()
    load_cot.wait()
    load_in.start()
    load_out.start()
    weight_row = jnp.maximum(cnt_ref[...], 1).astype(F32)
    diagonal = iota((toks, toks), 0) == iota((toks, toks), 1)
    weight = jnp.sum(jnp.where(diagonal, weight_row, 0.0), axis=1, keepdims=True)
    scaled = (cot_ref[...].astype(F32) * (1.0 / weight)).astype(BF16)

    pieces = SEG // (2 * SLOT)
    both = jnp.concatenate([tok, scaled], axis=0)
    total = jnp.zeros((wide, piece), F32)
    for part in range(pieces):
        low = part * piece
        high = min(width, low + piece)
        chosen = jnp.where(part_of == part, take, 0.0).astype(BF16)
        term = nn(chosen, both[:, low:high])
        if high - low < piece:
            term = jnp.concatenate([term, jnp.zeros((wide, piece - high + low), F32)], axis=1)
        total = total + term
    send[...] = total.astype(BF16).reshape(experts, SEG, piece)
    recv[pl.ds(me, 1)] = send[pl.ds(me, 1)]

    pl.semaphore_wait(barrier, experts - 1 + groups - 1)
    dispatch = exchange("expert", experts, me, lambda peer: send.at[peer], recv.at[me], d_ss, d_rs)

    load_router.wait()
    router = router_ref[...]
    stacked = jnp.concatenate(split3(router), axis=0).astype(BF16)
    parts = nt(stacked, tok)
    logits = parts[:experts] + parts[experts : 2 * experts] + parts[2 * experts :]
    raised = jnp.exp(logits - jnp.max(logits, axis=0, keepdims=True))
    prob = raised / jnp.sum(raised, axis=0, keepdims=True)
    padded = jnp.concatenate(
        split3(prob) + (jnp.zeros((LANES - 3 * experts, toks), F32),), axis=0
    )
    gate_s[...] = nt(hit.astype(BF16), padded.astype(BF16)).astype(BF16).reshape(experts, SEG, LANES)
    gate_r[pl.ds(me, 1)] = gate_s[pl.ds(me, 1)]
    send_gates = exchange("expert", experts, me, lambda peer: gate_s.at[peer], gate_r.at[me], g_ss, g_rs)

    mine = iota((experts, capacity), 0) == me
    owner_row = jnp.sum(jnp.where(mine, owner, 0), axis=0, keepdims=True)
    tall = 2 * capacity
    slot_row = iota((tall, capacity), 0) % capacity
    slot_col = iota((tall, capacity), 1)
    owner_col = jnp.sum(jnp.where(slot_row == slot_col, owner_row, 0), axis=1, keepdims=True)
    same = owner_col == owner_row
    rank_col = jnp.sum(jnp.where(same & (slot_col < slot_row), 1, 0), axis=1, keepdims=True)
    seat_c = iota((tall, wide), 1) % SEG
    is_dy = jnp.where(iota((tall, wide), 0) >= capacity, 1, 0)
    wanted = (iota((tall, wide), 1) // SEG == owner_col) & (
        seat_c % (2 * SLOT) == SLOT * is_dy + rank_col
    )
    blocks = [one_hot(wanted & (seat_c // (2 * SLOT) == part)) for part in range(pieces)]
    gate_block = one_hot(
        (iota((capacity, wide), 1) // SEG == owner_col[:capacity])
        & (iota((capacity, wide), 1) % SEG == rank_col[:capacity])
    )
    before = same[:capacity] & (slot_row[:capacity] < slot_col[:capacity])
    rank_row = jnp.sum(jnp.where(before, 1, 0), axis=0, keepdims=True)
    row_u = iota((wide, capacity), 0)
    from_owner = row_u // SEG == owner_row
    hit_turned = hit.T
    seat_turned = iota((toks, wide), 1) % SEG

    arrive(dispatch)
    rows_in = recv[...].reshape(wide, piece)
    packed = []
    for part in range(pieces):
        taken = min(width, (part + 1) * piece) - part * piece
        packed.append(nn(blocks[part], rows_in[:, :taken]))
    packed.append(jnp.zeros((tall, whole - width), F32))
    packed = jnp.concatenate(packed, axis=1)

    def folded(rows):
        return jnp.concatenate([rows[..., :half], rows[..., half:]], axis=-2).astype(BF16)

    def unfolded(pack):
        rows = pack[...].astype(F32)
        return jnp.concatenate([rows[:, :capacity], rows[:, capacity:]], axis=2).reshape(count, whole)

    pack_x[pl.ds(my_group, 1)] = folded(packed[:capacity])[None]
    gather_x = exchange(
        "dp", groups, my_group, lambda peer: pack_x.at[my_group], pack_x.at[my_group], x_ss, x_rs
    )
    arrive(send_gates)
    gate_rows = nn(gate_block, gate_r[...].reshape(wide, LANES))
    packed_d = [packed[capacity:, :width], gate_rows]
    if whole > width + LANES:
        packed_d.append(jnp.zeros((capacity, whole - width - LANES), F32))
    pack_d[pl.ds(my_group, 1)] = folded(jnp.concatenate(packed_d, axis=1))[None]
    gather_d = exchange(
        "dp", groups, my_group, lambda peer: pack_d.at[my_group], pack_d.at[my_group], y_ss, y_rs
    )
    load_in.wait()
    load_out.wait()
    arrive(gather_x)

    x_rows = unfolded(pack_x)[:, :width].astype(BF16)
    x_ref[...] = x_rows
    stores[0].start()
    step_cols = min(hidden, 256)
    for tile in range(hidden // step_cols):
        cols = slice(tile * step_cols, (tile + 1) * step_cols)
        pre = nn(x_rows, win[:, cols])
        cdf = normal_cdf(pre)
        act_ref[:, cols] = (pre * cdf).astype(BF16)
        slope_ref[:, cols] = cdf + pre * jnp.exp(-0.5 * pre * pre) * 0.3989422804014327
    stores[2].start()

    arrive(gather_d)
    dy_full = unfolded(pack_d)
    dy_wide = dy_full[:, :width]
    gate_lanes = dy_full[:, width : width + LANES]
    lane = iota((count, LANES), 1)
    gate = jnp.sum(jnp.where(lane == me, gate_lanes, 0.0), axis=1, keepdims=True)
    dy_rows = dy_wide.astype(BF16)
    gate_part = jnp.zeros((count, 1), F32)
    for tile in range(hidden // step_cols):
        cols = slice(tile * step_cols, (tile + 1) * step_cols)
        back_act = nt(dy_rows, wout[cols, :])
        pg_ref[:, cols] = (gate * back_act * slope_ref[:, cols]).astype(BF16)
        gate_part = gate_part + jnp.sum(act_ref[:, cols].astype(F32) * back_act, axis=1, keepdims=True)
    stores[3].start()
    og_ref[...] = (gate * dy_wide).astype(BF16)
    stores[1].start()

    pre_grad = pg_ref[...]

    def row_columns(low, high):
        return [
            nt(pre_grad, win[start : min(high, start + 256), :]) for start in range(low, high, 256)
        ]

    def to_groups(columns, sent, kept, send_sem, recv_sem):
        rows = jnp.concatenate(columns, axis=1).reshape(groups, capacity, 2 * sent.shape[2])
        side = sent.shape[2]
        sent[...] = jnp.concatenate([rows[:, :, :side], rows[:, :, side:]], axis=1).astype(BF16)
        kept[pl.ds(my_group, 1)] = sent[pl.ds(my_group, 1)]
        return exchange(
            "dp", groups, my_group, lambda peer: sent.at[peer], kept.at[my_group], send_sem, recv_sem
        )

    head_sum = to_groups(row_columns(0, head), head_s, head_r, h_ss, h_rs)
    g1, g2, g3 = split3(gate_part)
    tail = row_columns(head, width)
    tail.append(jnp.where(lane == 0, g1, jnp.where(lane == 1, g2, jnp.where(lane == 2, g3, 0.0))))
    spare = head + 2 * tail_s.shape[2] - width - LANES
    if spare:
        tail.append(jnp.zeros((count, spare), F32))
    tail_sum = to_groups(tail, tail_s, tail_r, r_ss, r_rs)

    fold_row, fold_col = iota((LANES, LANES), 0), iota((LANES, LANES), 1)
    fold = one_hot((fold_row % experts == fold_col) & (fold_row < 3 * experts))
    row_prob = nn(gate_lanes.astype(BF16), fold)
    own_prob = jnp.sum(jnp.where(lane == me, row_prob, 0.0), axis=1, keepdims=True)
    logit_part = gate_part * row_prob * (jnp.where(lane == me, 1.0, 0.0) - own_prob)
    term = tn(
        jnp.concatenate(split3(logit_part), axis=0).astype(BF16),
        jnp.concatenate([x_rows, x_rows, x_rows], axis=0),
    )[:experts]
    for part in range(experts):
        low = part * chunk
        high = min(width, low + chunk)
        if high <= low:
            term_s[part] = jnp.zeros((experts, chunk), F32)
            continue
        value = term[:, low:high]
        if high - low < chunk:
            value = jnp.concatenate([value, jnp.zeros((experts, chunk - high + low), F32)], axis=1)
        term_s[part] = value
    term_r[pl.ds(me, 1)] = term_s[pl.ds(me, 1)]
    scatter = exchange("expert", experts, me, lambda peer: term_s.at[peer], term_r.at[me], t_ss, t_rs)

    def over_blocks(kept):
        summed = kept[0].astype(F32)
        for group in range(1, groups):
            summed = summed + kept[group].astype(F32)
        return [summed[:capacity], summed[capacity:]]

    arrive(head_sum)
    row_sides = over_blocks(head_r)
    arrive(tail_sum)
    row_total = jnp.concatenate(row_sides + over_blocks(tail_r), axis=1)
    gate_total = jnp.sum(row_total[:, width : width + LANES], axis=1, keepdims=True)
    row_grad = jnp.concatenate(
        [
            row_total[:, :width],
            jnp.where(iota((capacity, LANES), 1) == me, gate_total, 0.0),
        ],
        axis=1,
    ).astype(BF16).astype(F32)
    returned = jnp.zeros((wide, back), F32)
    back_pieces = -(-(width + LANES) // back)
    for part in range(back_pieces):
        low = part * back
        high = min(width + LANES, low + back)
        give = jnp.where(from_owner & (row_u % SEG == SLOT * part + rank_row), 1.0, 0.0)
        term = nn(give, row_grad[:, low:high])
        if high - low < back:
            term = jnp.concatenate([term, jnp.zeros((wide, back - high + low), F32)], axis=1)
        returned = returned + term
    ret_s[...] = returned.astype(BF16).reshape(experts, SEG, back)
    ret_r[pl.ds(me, 1)] = ret_s[pl.ds(me, 1)]
    give_back = exchange("expert", experts, me, lambda peer: ret_s.at[peer], ret_r.at[me], b_ss, b_rs)

    arrive(scatter)
    term_sum = term_r[0]
    for part in range(1, experts):
        term_sum = term_sum + term_r[part]
    sum_r[pl.ds(my_group, 1)] = term_sum[None]
    over_dp = exchange("dp", groups, my_group, lambda peer: sum_r.at[my_group], sum_r.at[my_group], s_ss, s_rs)

    marks = [
        jnp.where(seat_turned // SLOT == part, hit_turned, 0.0).astype(BF16)
        for part in range(back_pieces)
    ]
    r1, r2, r3 = split3(router)
    near = jnp.concatenate([r1, r2, r1, r3, r1, r2], axis=0).astype(BF16)

    arrive(over_dp)
    final = sum_r[0]
    for group in range(1, groups):
        final = final + sum_r[group]
    fin_r[pl.ds(me, 1)] = final[None]
    spread_out = exchange("expert", experts, me, lambda peer: fin_r.at[me], fin_r.at[me], f_ss, f_rs)

    arrive(give_back)
    ret_rows = ret_r[...].reshape(wide, back)
    gate_low = width - (back_pieces - 1) * back
    prob_grad = nt(
        ret_rows[:, gate_low : gate_low + LANES].T, marks[back_pieces - 1]
    )[:experts]
    logit_grad = prob * (prob_grad - jnp.sum(prob * prob_grad, axis=0, keepdims=True))
    l1, l2, l3 = split3(logit_grad)
    left = jnp.concatenate([l1, l1, l2, l1, l3, l2], axis=0).astype(BF16)
    gt_wide = tn(left, near)
    for part in range(back_pieces):
        low = part * back
        high = min(width, low + back)
        expert_sum = nn(marks[part], ret_rows[:, : high - low])
        gt_ref[:, low:high] = (expert_sum + gt_wide[:, low:high]).astype(BF16)

    stores[4].start()

    arrive(spread_out)
    for part in range(experts):
        low = part * chunk
        high = min(width, low + chunk)
        if high > low:
            gr_ref[:, low:high] = fin_r[part][:, : high - low]
    stores[5].start()
    for store in stores:
        store.wait()
    for copies in (dispatch, send_gates, gather_x, gather_d, head_sum, tail_sum, give_back, scatter, over_dp, spread_out):
        for copy in copies:
            copy.wait_send()


def weight_kernel(
    x_hbm, og_hbm, act_hbm, pg_hbm, gt_in, gr_in, gt_hbm, gin_hbm, gout_hbm, gr_hbm,
    x_ref, og_ref, act_ref, pg_ref, gt_ref, gr_ref, gin_ref, gout_ref, in_sem, out_sem,
):
    loads = []
    for source, target in (
        (x_hbm, x_ref), (pg_hbm, pg_ref), (act_hbm, act_ref), (og_hbm, og_ref), (gt_in, gt_ref), (gr_in, gr_ref)
    ):
        loads.append(pltpu.make_async_copy(source, target, in_sem.at[len(loads)]))
        loads[-1].start()
    stores = []

    def product(left, right, held, target):
        rows = held.shape[0]
        for low in range(0, rows, 256):
            span = slice(low, min(rows, low + 256))
            held[span, :] = tn(left[:, span], right[...]).astype(BF16)
            stores.append(pltpu.make_async_copy(held.at[span], target.at[0, span], out_sem.at[len(stores)]))
            stores[-1].start()

    loads[0].wait()
    loads[1].wait()
    product(x_ref, pg_ref, gin_ref, gin_hbm)
    for load, held, target in ((loads[4], gt_ref, gt_hbm), (loads[5], gr_ref, gr_hbm)):
        load.wait()
        stores.append(pltpu.make_async_copy(held, target, out_sem.at[len(stores)]))
        stores[-1].start()
    loads[2].wait()
    loads[3].wait()
    product(act_ref, og_ref, gout_ref, gout_hbm)
    for store in stores:
        store.wait()


def shards(experts, groups, tokens, cotangent, counts, picks, router, w_in, w_out):
    toks, width = tokens.shape
    capacity = picks.shape[2]
    hidden = w_in.shape[2]
    count = groups * capacity
    tiles = -(-width // LANES)
    pieces = SEG // (2 * SLOT)
    piece = LANES * -(-tiles // pieces)
    half = LANES * -(-(tiles + 1) // 2)
    back = LANES * -(-(tiles + 1) // (SEG // SLOT))
    head = LANES * ((tiles + 1) * 2 // 7)
    tail = half - head
    chunk = LANES * -(-tiles // experts)
    hbm = pl.BlockSpec(memory_space=pltpu.HBM)
    dma = pltpu.SemaphoreType.DMA
    over_e, over_g = dma((experts,)), dma((groups,))
    row_scratch = [
        pltpu.VMEM((count, width), BF16),
        pltpu.VMEM((count, width), BF16),
    ]
    results = pl.pallas_call(
        functools.partial(route_kernel, experts, groups),
        out_shape=(
            jax.ShapeDtypeStruct((count, width), BF16),
            jax.ShapeDtypeStruct((count, width), BF16),
            jax.ShapeDtypeStruct((count, hidden), BF16),
            jax.ShapeDtypeStruct((count, hidden), BF16),
            jax.ShapeDtypeStruct((toks, width), BF16),
            jax.ShapeDtypeStruct((experts, width), F32),
        ),
        in_specs=[hbm] * 7,
        out_specs=(hbm,) * 6,
        scratch_shapes=row_scratch
        + [
            pltpu.VMEM((toks, width), BF16),
            pltpu.VMEM((experts, width), F32),
            pltpu.VMEM((toks, width), BF16),
            pltpu.VMEM((toks, width), BF16),
            pltpu.VMEM((1, toks), jnp.int32),
            pltpu.VMEM((experts, capacity), jnp.int32),
            pltpu.VMEM((experts, width), F32),
            pltpu.VMEM((width, hidden), BF16),
            pltpu.VMEM((hidden, width), BF16),
            pltpu.VMEM((experts, SEG, piece), BF16),
            pltpu.VMEM((experts, SEG, piece), BF16),
            pltpu.VMEM((experts, SEG, LANES), BF16),
            pltpu.VMEM((experts, SEG, LANES), BF16),
            pltpu.VMEM((groups, 2 * capacity, half), BF16),
            pltpu.VMEM((groups, 2 * capacity, half), BF16),
            pltpu.VMEM((count, hidden), BF16),
            pltpu.VMEM((count, hidden), BF16),
            pltpu.VMEM((count, hidden), F32),
            pltpu.VMEM((groups, 2 * capacity, head), BF16),
            pltpu.VMEM((groups, 2 * capacity, head), BF16),
            pltpu.VMEM((groups, 2 * capacity, tail), BF16),
            pltpu.VMEM((groups, 2 * capacity, tail), BF16),
            pltpu.VMEM((experts, SEG, back), BF16),
            pltpu.VMEM((experts, SEG, back), BF16),
            pltpu.VMEM((experts, experts, chunk), F32),
            pltpu.VMEM((experts, experts, chunk), F32),
            pltpu.VMEM((groups, experts, chunk), F32),
            pltpu.VMEM((experts, experts, chunk), F32),
            dma((7,)),
            dma((6,)),
            over_e, over_e,
            over_e, over_e,
            over_g, over_g,
            over_g, over_g,
            over_g, over_g,
            over_g, over_g,
            over_e, over_e,
            over_e, over_e,
            over_g, over_g,
            over_e, over_e,
        ],
        compiler_params=pltpu.CompilerParams(
            collective_id=0, has_side_effects=True, vmem_limit_bytes=58 * 1024 * 1024
        ),
        name="route",
    )(tokens, cotangent, counts.reshape(1, toks), picks[0], router.T, w_in[0], w_out[0])

    grad_tokens, grad_in, grad_out, grad_router = pl.pallas_call(
        weight_kernel,
        out_shape=(
            jax.ShapeDtypeStruct((toks, width), BF16),
            jax.ShapeDtypeStruct((1, width, hidden), BF16),
            jax.ShapeDtypeStruct((1, hidden, width), BF16),
            jax.ShapeDtypeStruct((experts, width), F32),
        ),
        in_specs=[hbm] * 6,
        out_specs=(hbm,) * 4,
        scratch_shapes=row_scratch
        + [
            pltpu.VMEM((count, hidden), BF16),
            pltpu.VMEM((count, hidden), BF16),
            pltpu.VMEM((toks, width), BF16),
            pltpu.VMEM((experts, width), F32),
            pltpu.VMEM((width, hidden), BF16),
            pltpu.VMEM((hidden, width), BF16),
            dma((6,)),
            dma((-(-width // 256) + -(-hidden // 256) + 2,)),
        ],
        compiler_params=pltpu.CompilerParams(vmem_limit_bytes=58 * 1024 * 1024),
        name="weight_grads",
    )(*results)
    return grad_tokens, grad_in, grad_out, grad_router.T


def solution(mesh):
    placed = (
        P(("dp", "expert"), None),
        P(("dp", "expert"), None),
        P(("dp", "expert")),
        P("dp", None, None),
        P(),
        P("expert", None, "dp"),
        P("expert", "dp", None),
    )
    return jax.shard_map(
        functools.partial(shards, mesh.shape["expert"], mesh.shape["dp"]),
        mesh=mesh,
        in_specs=placed,
        out_specs=(
            P(("dp", "expert"), None),
            P("expert", None, "dp"),
            P("expert", "dp", None),
            P(),
        ),
        check_vma=False,
    )
```

```python
import functools

import jax
import jax.numpy as jnp
from jax import lax
from jax.experimental import pallas as pl
from jax.experimental.pallas import tpu as pltpu
from jax.sharding import PartitionSpec as P

MESH = pl.DeviceIdType.MESH
BF16 = jnp.bfloat16
F32 = jnp.float32
SLOT = 2
SEG = 16
LANES = 128


def nn(left, right):
    return lax.dot_general(left, right, (((1,), (0,)), ((), ())), preferred_element_type=F32)


def nt(left, right):
    return lax.dot_general(left, right, (((1,), (1,)), ((), ())), preferred_element_type=F32)


def tn(left, right):
    return lax.dot_general(left, right, (((0,), (0,)), ((), ())), preferred_element_type=F32)


def iota(shape, dim):
    return lax.broadcasted_iota(jnp.int32, shape, dim)


def one_hot(mask):
    return jnp.where(mask, 1.0, 0.0).astype(BF16)


def split3(values):
    high = values.astype(BF16).astype(F32)
    rest = values - high
    mid = rest.astype(BF16).astype(F32)
    return high, mid, rest - mid


def normal_cdf(values):
    return 0.5 * (1.0 + lax.erf(values * 0.7071067811865476))


def exchange(axis, count, me, source, target, send_sem, recv_sem):
    copies = []
    for step in range(1, count):
        peer = lax.rem(me + step, count)
        copy = pltpu.make_async_remote_copy(
            src_ref=source(peer),
            dst_ref=target,
            send_sem=send_sem.at[step],
            recv_sem=recv_sem.at[step],
            device_id={axis: peer},
            device_id_type=MESH,
        )
        copy.start()
        copies.append(copy)
    return copies


def arrive(copies):
    for copy in copies:
        copy.wait_recv()


def route_kernel(
    experts, groups, tok_hbm, cot_hbm, cnt_hbm, pick_hbm, router_hbm, win_hbm, wout_hbm,
    x_hbm, og_hbm, act_hbm, pg_hbm, gt_hbm, gr_hbm,
    x_ref, og_ref, gt_ref, gr_ref, tok_ref, cot_ref, cnt_ref, pick_ref, router_ref, win, wout,
    send, recv, gate_s, gate_r, pack_x, pack_d, act_ref, pg_ref, slope_ref, head_s, head_r, tail_s, tail_r, ret_s, ret_r,
    term_s, term_r, sum_r, fin_r,
    in_sem, out_sem, d_ss, d_rs, g_ss, g_rs, x_ss, x_rs, y_ss, y_rs, h_ss, h_rs, r_ss, r_rs, b_ss, b_rs, t_ss, t_rs, s_ss, s_rs, f_ss, f_rs,
):
    me = lax.axis_index("expert")
    my_group = lax.axis_index("dp")
    toks, width = tok_ref.shape
    capacity = pick_ref.shape[1]
    hidden = win.shape[1]
    count = groups * capacity
    piece = send.shape[2]
    half = pack_x.shape[2]
    whole = 2 * half
    head = 2 * head_s.shape[2]
    back = ret_s.shape[2]
    chunk = term_s.shape[2]
    back_pieces = -(-(width + LANES) // back)

    barrier = pltpu.get_barrier_semaphore()
    for step in range(1, experts):
        pl.semaphore_signal(
            barrier, inc=1, device_id={"expert": lax.rem(me + step, experts)}, device_id_type=MESH
        )
    for step in range(1, groups):
        pl.semaphore_signal(
            barrier, inc=1, device_id={"dp": lax.rem(my_group + step, groups)}, device_id_type=MESH
        )
    loads = []
    for source, target in (
        (pick_hbm, pick_ref), (tok_hbm, tok_ref), (router_hbm, router_ref), (cnt_hbm, cnt_ref),
        (cot_hbm, cot_ref), (win_hbm, win), (wout_hbm, wout),
    ):
        loads.append(pltpu.make_async_copy(source, target, in_sem.at[len(loads)]))
    stores = []
    for source, target in (
        (x_ref, x_hbm), (og_ref, og_hbm), (act_ref, act_hbm), (pg_ref, pg_hbm), (gt_ref, gt_hbm), (gr_ref, gr_hbm)
    ):
        stores.append(pltpu.make_async_copy(source, target, out_sem.at[len(stores)]))
    load_pick, load_tok, load_router, load_cnt, load_cot, load_in, load_out = loads
    for load in loads[:5]:
        load.start()

    load_pick.wait()
    picks = pick_ref[...]
    owner = picks // toks
    place = picks - owner * toks
    codes = jnp.concatenate([owner, place], axis=1).astype(F32).astype(BF16)
    wide = experts * SEG
    spread = one_hot(iota((wide, experts), 0) // SEG == iota((wide, experts), 1))
    spread_codes = nn(spread, codes)
    held = spread_codes[:, :capacity] == me.astype(F32)
    spots = spread_codes[:, capacity:]
    first = jnp.min(jnp.where(held, spots, 1e6), axis=1, keepdims=True)
    last = jnp.max(jnp.where(held, spots, -1.0), axis=1, keepdims=True)
    last = jnp.where(last > first, last, -1.0)
    seat = iota((wide, toks), 0) % SEG
    token_id = iota((wide, toks), 1).astype(F32)
    hit = (token_id == jnp.where(seat % SLOT == 0, first, last)).astype(F32)
    late = seat % (2 * SLOT) >= SLOT
    take = jnp.concatenate([jnp.where(late, 0.0, hit), jnp.where(late, hit, 0.0)], axis=1)
    part_of = iota((wide, 2 * toks), 0) % SEG // (2 * SLOT)

    load_tok.wait()
    tok = tok_ref[...]
    load_cnt.wait()
    load_cot.wait()
    load_in.start()
    load_out.start()
    weight_row = jnp.maximum(cnt_ref[...], 1).astype(F32)
    diagonal = iota((toks, toks), 0) == iota((toks, toks), 1)
    weight = jnp.sum(jnp.where(diagonal, weight_row, 0.0), axis=1, keepdims=True)
    scaled = (cot_ref[...].astype(F32) * (1.0 / weight)).astype(BF16)

    pieces = SEG // (2 * SLOT)
    both = jnp.concatenate([tok, scaled], axis=0)
    total = jnp.zeros((wide, piece), F32)
    for part in range(pieces):
        low = part * piece
        high = min(width, low + piece)
        chosen = jnp.where(part_of == part, take, 0.0).astype(BF16)
        term = nn(chosen, both[:, low:high])
        if high - low < piece:
            term = jnp.concatenate([term, jnp.zeros((wide, piece - high + low), F32)], axis=1)
        total = total + term
    send[...] = total.astype(BF16).reshape(experts, SEG, piece)
    recv[pl.ds(me, 1)] = send[pl.ds(me, 1)]

    pl.semaphore_wait(barrier, experts - 1 + groups - 1)
    dispatch = exchange("expert", experts, me, lambda peer: send.at[peer], recv.at[me], d_ss, d_rs)

    load_router.wait()
    router = router_ref[...]
    stacked = jnp.concatenate(split3(router), axis=0).astype(BF16)
    parts = nt(stacked, tok)
    logits = parts[:experts] + parts[experts : 2 * experts] + parts[2 * experts :]
    raised = jnp.exp(logits - jnp.max(logits, axis=0, keepdims=True))
    prob = raised / jnp.sum(raised, axis=0, keepdims=True)
    padded = jnp.concatenate(
        split3(prob) + (jnp.zeros((LANES - 3 * experts, toks), F32),), axis=0
    )
    gate_s[...] = nt(hit.astype(BF16), padded.astype(BF16)).astype(BF16).reshape(experts, SEG, LANES)
    gate_r[pl.ds(me, 1)] = gate_s[pl.ds(me, 1)]
    send_gates = exchange("expert", experts, me, lambda peer: gate_s.at[peer], gate_r.at[me], g_ss, g_rs)

    mine = iota((experts, capacity), 0) == me
    owner_row = jnp.sum(jnp.where(mine, owner, 0), axis=0, keepdims=True)
    tall = 2 * capacity
    slot_row = iota((tall, capacity), 0) % capacity
    slot_col = iota((tall, capacity), 1)
    owner_col = jnp.sum(jnp.where(slot_row == slot_col, owner_row, 0), axis=1, keepdims=True)
    same = owner_col == owner_row
    rank_col = jnp.sum(jnp.where(same & (slot_col < slot_row), 1, 0), axis=1, keepdims=True)
    seat_c = iota((tall, wide), 1) % SEG
    is_dy = jnp.where(iota((tall, wide), 0) >= capacity, 1, 0)
    wanted = (iota((tall, wide), 1) // SEG == owner_col) & (
        seat_c % (2 * SLOT) == SLOT * is_dy + rank_col
    )
    blocks = [one_hot(wanted & (seat_c // (2 * SLOT) == part)) for part in range(pieces)]
    gate_block = one_hot(
        (iota((capacity, wide), 1) // SEG == owner_col[:capacity])
        & (iota((capacity, wide), 1) % SEG == rank_col[:capacity])
    )
    before = same[:capacity] & (slot_row[:capacity] < slot_col[:capacity])
    rank_row = jnp.sum(jnp.where(before, 1, 0), axis=0, keepdims=True)
    row_u = iota((wide, capacity), 0)
    from_owner = row_u // SEG == owner_row
    hit_turned = hit.T
    seat_turned = iota((toks, wide), 1) % SEG

    arrive(dispatch)
    rows_in = recv[...].reshape(wide, piece)
    packed = []
    for part in range(pieces):
        taken = min(width, (part + 1) * piece) - part * piece
        packed.append(nn(blocks[part], rows_in[:, :taken]))
    packed.append(jnp.zeros((tall, whole - width), F32))
    packed = jnp.concatenate(packed, axis=1)

    def folded(rows):
        return jnp.concatenate([rows[..., :half], rows[..., half:]], axis=-2).astype(BF16)

    def unfolded(pack):
        rows = pack[...].astype(F32)
        return jnp.concatenate([rows[:, :capacity], rows[:, capacity:]], axis=2).reshape(count, whole)

    pack_x[pl.ds(my_group, 1)] = folded(packed[:capacity])[None]
    gather_x = exchange(
        "dp", groups, my_group, lambda peer: pack_x.at[my_group], pack_x.at[my_group], x_ss, x_rs
    )
    arrive(send_gates)
    gate_rows = nn(gate_block, gate_r[...].reshape(wide, LANES))
    packed_d = [packed[capacity:, :width], gate_rows]
    if whole > width + LANES:
        packed_d.append(jnp.zeros((capacity, whole - width - LANES), F32))
    pack_d[pl.ds(my_group, 1)] = folded(jnp.concatenate(packed_d, axis=1))[None]
    gather_d = exchange(
        "dp", groups, my_group, lambda peer: pack_d.at[my_group], pack_d.at[my_group], y_ss, y_rs
    )
    load_in.wait()
    load_out.wait()
    arrive(gather_x)

    x_rows = unfolded(pack_x)[:, :width].astype(BF16)
    x_ref[...] = x_rows
    stores[0].start()
    step_cols = min(hidden, 256)
    for tile in range(hidden // step_cols):
        cols = slice(tile * step_cols, (tile + 1) * step_cols)
        pre = nn(x_rows, win[:, cols])
        cdf = normal_cdf(pre)
        act_ref[:, cols] = (pre * cdf).astype(BF16)
        slope_ref[:, cols] = cdf + pre * jnp.exp(-0.5 * pre * pre) * 0.3989422804014327
    stores[2].start()

    arrive(gather_d)
    dy_full = unfolded(pack_d)
    dy_wide = dy_full[:, :width]
    gate_lanes = dy_full[:, width : width + LANES]
    lane = iota((count, LANES), 1)
    gate = jnp.sum(jnp.where(lane == me, gate_lanes, 0.0), axis=1, keepdims=True)
    dy_rows = dy_wide.astype(BF16)
    gate_part = jnp.zeros((count, 1), F32)
    for tile in range(hidden // step_cols):
        cols = slice(tile * step_cols, (tile + 1) * step_cols)
        back_act = nt(dy_rows, wout[cols, :])
        pg_ref[:, cols] = (gate * back_act * slope_ref[:, cols]).astype(BF16)
        gate_part = gate_part + jnp.sum(act_ref[:, cols].astype(F32) * back_act, axis=1, keepdims=True)
    stores[3].start()
    og_ref[...] = (gate * dy_wide).astype(BF16)
    stores[1].start()

    pre_grad = pg_ref[...]

    def row_columns(low, high):
        return [
            nt(pre_grad, win[start : min(high, start + 256), :]) for start in range(low, high, 256)
        ]

    def to_groups(columns, sent, kept, send_sem, recv_sem):
        rows = jnp.concatenate(columns, axis=1).reshape(groups, capacity, 2 * sent.shape[2])
        side = sent.shape[2]
        sent[...] = jnp.concatenate([rows[:, :, :side], rows[:, :, side:]], axis=1).astype(BF16)
        kept[pl.ds(my_group, 1)] = sent[pl.ds(my_group, 1)]
        return exchange(
            "dp", groups, my_group, lambda peer: sent.at[peer], kept.at[my_group], send_sem, recv_sem
        )

    head_sum = to_groups(row_columns(0, head), head_s, head_r, h_ss, h_rs)
    fold_row, fold_col = iota((LANES, LANES), 0), iota((LANES, LANES), 1)
    fold = one_hot((fold_row % experts == fold_col) & (fold_row < 3 * experts))
    row_prob = nn(gate_lanes.astype(BF16), fold)
    own_prob = jnp.sum(jnp.where(lane == me, row_prob, 0.0), axis=1, keepdims=True)
    logit_part = gate_part * row_prob * (jnp.where(lane == me, 1.0, 0.0) - own_prob)
    term = tn(
        jnp.concatenate(split3(logit_part), axis=0).astype(BF16),
        jnp.concatenate([x_rows, x_rows, x_rows], axis=0),
    )[:experts]
    for part in range(experts):
        low = part * chunk
        high = min(width, low + chunk)
        if high <= low:
            term_s[part] = jnp.zeros((experts, chunk), F32)
            continue
        value = term[:, low:high]
        if high - low < chunk:
            value = jnp.concatenate([value, jnp.zeros((experts, chunk - high + low), F32)], axis=1)
        term_s[part] = value
    term_r[pl.ds(me, 1)] = term_s[pl.ds(me, 1)]
    scatter = exchange("expert", experts, me, lambda peer: term_s.at[peer], term_r.at[me], t_ss, t_rs)

    g1, g2, g3 = split3(gate_part)
    tail = row_columns(head, width)
    tail.append(jnp.where(lane == 0, g1, jnp.where(lane == 1, g2, jnp.where(lane == 2, g3, 0.0))))
    spare = head + 2 * tail_s.shape[2] - width - LANES
    if spare:
        tail.append(jnp.zeros((count, spare), F32))
    tail_sum = to_groups(tail, tail_s, tail_r, r_ss, r_rs)

    def over_blocks(kept):
        summed = kept[0].astype(F32)
        for group in range(1, groups):
            summed = summed + kept[group].astype(F32)
        return [summed[:capacity], summed[capacity:]]

    arrive(scatter)
    term_sum = term_r[0]
    for part in range(1, experts):
        term_sum = term_sum + term_r[part]
    sum_r[pl.ds(my_group, 1)] = term_sum[None]
    over_dp = exchange("dp", groups, my_group, lambda peer: sum_r.at[my_group], sum_r.at[my_group], s_ss, s_rs)

    marks = [
        jnp.where(seat_turned // SLOT == part, hit_turned, 0.0).astype(BF16)
        for part in range(back_pieces)
    ]
    r1, r2, r3 = split3(router)
    near = jnp.concatenate([r1, r2, r1, r3, r1, r2], axis=0).astype(BF16)

    arrive(head_sum)
    row_sides = over_blocks(head_r)
    arrive(tail_sum)
    row_total = jnp.concatenate(row_sides + over_blocks(tail_r), axis=1)
    gate_total = jnp.sum(row_total[:, width : width + LANES], axis=1, keepdims=True)
    row_grad = jnp.concatenate(
        [
            row_total[:, :width],
            jnp.where(iota((capacity, LANES), 1) == me, gate_total, 0.0),
        ],
        axis=1,
    ).astype(BF16).astype(F32)
    returned = jnp.zeros((wide, back), F32)
    for part in range(back_pieces):
        low = part * back
        high = min(width + LANES, low + back)
        give = jnp.where(from_owner & (row_u % SEG == SLOT * part + rank_row), 1.0, 0.0)
        term = nn(give, row_grad[:, low:high])
        if high - low < back:
            term = jnp.concatenate([term, jnp.zeros((wide, back - high + low), F32)], axis=1)
        returned = returned + term
    ret_s[...] = returned.astype(BF16).reshape(experts, SEG, back)
    ret_r[pl.ds(me, 1)] = ret_s[pl.ds(me, 1)]
    give_back = exchange("expert", experts, me, lambda peer: ret_s.at[peer], ret_r.at[me], b_ss, b_rs)

    arrive(over_dp)
    final = sum_r[0]
    for group in range(1, groups):
        final = final + sum_r[group]
    fin_r[pl.ds(me, 1)] = final[None]
    spread_out = exchange("expert", experts, me, lambda peer: fin_r.at[me], fin_r.at[me], f_ss, f_rs)

    arrive(give_back)
    ret_rows = ret_r[...].reshape(wide, back)
    gate_low = width - (back_pieces - 1) * back
    prob_grad = nt(
        ret_rows[:, gate_low : gate_low + LANES].T, marks[back_pieces - 1]
    )[:experts]
    logit_grad = prob * (prob_grad - jnp.sum(prob * prob_grad, axis=0, keepdims=True))
    l1, l2, l3 = split3(logit_grad)
    left = jnp.concatenate([l1, l1, l2, l1, l3, l2], axis=0).astype(BF16)
    gt_wide = tn(left, near)
    for part in range(back_pieces):
        low = part * back
        high = min(width, low + back)
        expert_sum = nn(marks[part], ret_rows[:, : high - low])
        gt_ref[:, low:high] = (expert_sum + gt_wide[:, low:high]).astype(BF16)

    stores[4].start()

    arrive(spread_out)
    for part in range(experts):
        low = part * chunk
        high = min(width, low + chunk)
        if high > low:
            gr_ref[:, low:high] = fin_r[part][:, : high - low]
    stores[5].start()
    for store in stores:
        store.wait()
    for copies in (dispatch, send_gates, gather_x, gather_d, head_sum, tail_sum, give_back, scatter, over_dp, spread_out):
        for copy in copies:
            copy.wait_send()


def weight_kernel(
    x_hbm, og_hbm, act_hbm, pg_hbm, gt_in, gr_in, gt_hbm, gin_hbm, gout_hbm, gr_hbm,
    x_ref, og_ref, act_ref, pg_ref, gt_ref, gr_ref, gin_ref, gout_ref, in_sem, out_sem,
):
    loads = []
    for source, target in (
        (x_hbm, x_ref), (pg_hbm, pg_ref), (act_hbm, act_ref), (og_hbm, og_ref), (gt_in, gt_ref), (gr_in, gr_ref)
    ):
        loads.append(pltpu.make_async_copy(source, target, in_sem.at[len(loads)]))
        loads[-1].start()
    stores = []

    def product(left, right, held, target):
        rows = held.shape[0]
        for low in range(0, rows, 256):
            span = slice(low, min(rows, low + 256))
            held[span, :] = tn(left[:, span], right[...]).astype(BF16)
            stores.append(pltpu.make_async_copy(held.at[span], target.at[0, span], out_sem.at[len(stores)]))
            stores[-1].start()

    loads[0].wait()
    loads[1].wait()
    product(x_ref, pg_ref, gin_ref, gin_hbm)
    for load, held, target in ((loads[4], gt_ref, gt_hbm), (loads[5], gr_ref, gr_hbm)):
        load.wait()
        stores.append(pltpu.make_async_copy(held, target, out_sem.at[len(stores)]))
        stores[-1].start()
    loads[2].wait()
    loads[3].wait()
    product(act_ref, og_ref, gout_ref, gout_hbm)
    for store in stores:
        store.wait()


def shards(experts, groups, tokens, cotangent, counts, picks, router, w_in, w_out):
    toks, width = tokens.shape
    capacity = picks.shape[2]
    hidden = w_in.shape[2]
    count = groups * capacity
    tiles = -(-width // LANES)
    pieces = SEG // (2 * SLOT)
    piece = LANES * -(-tiles // pieces)
    half = LANES * -(-(tiles + 1) // 2)
    back = LANES * -(-(tiles + 1) // (SEG // SLOT))
    head = LANES * ((tiles + 1) * 2 // 7)
    tail = half - head
    chunk = LANES * -(-tiles // experts)
    hbm = pl.BlockSpec(memory_space=pltpu.HBM)
    dma = pltpu.SemaphoreType.DMA
    over_e, over_g = dma((experts,)), dma((groups,))
    row_scratch = [
        pltpu.VMEM((count, width), BF16),
        pltpu.VMEM((count, width), BF16),
    ]
    results = pl.pallas_call(
        functools.partial(route_kernel, experts, groups),
        out_shape=(
            jax.ShapeDtypeStruct((count, width), BF16),
            jax.ShapeDtypeStruct((count, width), BF16),
            jax.ShapeDtypeStruct((count, hidden), BF16),
            jax.ShapeDtypeStruct((count, hidden), BF16),
            jax.ShapeDtypeStruct((toks, width), BF16),
            jax.ShapeDtypeStruct((experts, width), F32),
        ),
        in_specs=[hbm] * 7,
        out_specs=(hbm,) * 6,
        scratch_shapes=row_scratch
        + [
            pltpu.VMEM((toks, width), BF16),
            pltpu.VMEM((experts, width), F32),
            pltpu.VMEM((toks, width), BF16),
            pltpu.VMEM((toks, width), BF16),
            pltpu.VMEM((1, toks), jnp.int32),
            pltpu.VMEM((experts, capacity), jnp.int32),
            pltpu.VMEM((experts, width), F32),
            pltpu.VMEM((width, hidden), BF16),
            pltpu.VMEM((hidden, width), BF16),
            pltpu.VMEM((experts, SEG, piece), BF16),
            pltpu.VMEM((experts, SEG, piece), BF16),
            pltpu.VMEM((experts, SEG, LANES), BF16),
            pltpu.VMEM((experts, SEG, LANES), BF16),
            pltpu.VMEM((groups, 2 * capacity, half), BF16),
            pltpu.VMEM((groups, 2 * capacity, half), BF16),
            pltpu.VMEM((count, hidden), BF16),
            pltpu.VMEM((count, hidden), BF16),
            pltpu.VMEM((count, hidden), F32),
            pltpu.VMEM((groups, 2 * capacity, head), BF16),
            pltpu.VMEM((groups, 2 * capacity, head), BF16),
            pltpu.VMEM((groups, 2 * capacity, tail), BF16),
            pltpu.VMEM((groups, 2 * capacity, tail), BF16),
            pltpu.VMEM((experts, SEG, back), BF16),
            pltpu.VMEM((experts, SEG, back), BF16),
            pltpu.VMEM((experts, experts, chunk), F32),
            pltpu.VMEM((experts, experts, chunk), F32),
            pltpu.VMEM((groups, experts, chunk), F32),
            pltpu.VMEM((experts, experts, chunk), F32),
            dma((7,)),
            dma((6,)),
            over_e, over_e,
            over_e, over_e,
            over_g, over_g,
            over_g, over_g,
            over_g, over_g,
            over_g, over_g,
            over_e, over_e,
            over_e, over_e,
            over_g, over_g,
            over_e, over_e,
        ],
        compiler_params=pltpu.CompilerParams(
            collective_id=0, has_side_effects=True, vmem_limit_bytes=58 * 1024 * 1024
        ),
        name="route",
    )(tokens, cotangent, counts.reshape(1, toks), picks[0], router.T, w_in[0], w_out[0])

    grad_tokens, grad_in, grad_out, grad_router = pl.pallas_call(
        weight_kernel,
        out_shape=(
            jax.ShapeDtypeStruct((toks, width), BF16),
            jax.ShapeDtypeStruct((1, width, hidden), BF16),
            jax.ShapeDtypeStruct((1, hidden, width), BF16),
            jax.ShapeDtypeStruct((experts, width), F32),
        ),
        in_specs=[hbm] * 6,
        out_specs=(hbm,) * 4,
        scratch_shapes=row_scratch
        + [
            pltpu.VMEM((count, hidden), BF16),
            pltpu.VMEM((count, hidden), BF16),
            pltpu.VMEM((toks, width), BF16),
            pltpu.VMEM((experts, width), F32),
            pltpu.VMEM((width, hidden), BF16),
            pltpu.VMEM((hidden, width), BF16),
            dma((6,)),
            dma((-(-width // 256) + -(-hidden // 256) + 2,)),
        ],
        compiler_params=pltpu.CompilerParams(vmem_limit_bytes=58 * 1024 * 1024),
        name="weight_grads",
    )(*results)
    return grad_tokens, grad_in, grad_out, grad_router.T


def solution(mesh):
    placed = (
        P(("dp", "expert"), None),
        P(("dp", "expert"), None),
        P(("dp", "expert")),
        P("dp", None, None),
        P(),
        P("expert", None, "dp"),
        P("expert", "dp", None),
    )
    return jax.shard_map(
        functools.partial(shards, mesh.shape["expert"], mesh.shape["dp"]),
        mesh=mesh,
        in_specs=placed,
        out_specs=(
            P(("dp", "expert"), None),
            P("expert", None, "dp"),
            P("expert", "dp", None),
            P(),
        ),
        check_vma=False,
    )
```

```python
import functools

import jax
import jax.numpy as jnp
from jax import lax
from jax.experimental import pallas as pl
from jax.experimental.pallas import tpu as pltpu
from jax.sharding import PartitionSpec as P

MESH = pl.DeviceIdType.MESH
BF16 = jnp.bfloat16
F32 = jnp.float32
SLOT = 2
SEG = 16
LANES = 128


def nn(left, right):
    return lax.dot_general(left, right, (((1,), (0,)), ((), ())), preferred_element_type=F32)


def nt(left, right):
    return lax.dot_general(left, right, (((1,), (1,)), ((), ())), preferred_element_type=F32)


def tn(left, right):
    return lax.dot_general(left, right, (((0,), (0,)), ((), ())), preferred_element_type=F32)


def iota(shape, dim):
    return lax.broadcasted_iota(jnp.int32, shape, dim)


def one_hot(mask):
    return jnp.where(mask, 1.0, 0.0).astype(BF16)


def split3(values):
    high = values.astype(BF16).astype(F32)
    rest = values - high
    mid = rest.astype(BF16).astype(F32)
    return high, mid, rest - mid


def normal_cdf(values):
    return 0.5 * (1.0 + lax.erf(values * 0.7071067811865476))


def exchange(axis, count, me, source, target, send_sem, recv_sem):
    copies = []
    for step in range(1, count):
        peer = lax.rem(me + step, count)
        copy = pltpu.make_async_remote_copy(
            src_ref=source(peer),
            dst_ref=target,
            send_sem=send_sem.at[step],
            recv_sem=recv_sem.at[step],
            device_id={axis: peer},
            device_id_type=MESH,
        )
        copy.start()
        copies.append(copy)
    return copies


def arrive(copies):
    for copy in copies:
        copy.wait_recv()


def route_kernel(
    experts, groups, tok_hbm, cot_hbm, cnt_hbm, pick_hbm, router_hbm, win_hbm, wout_hbm,
    x_hbm, og_hbm, act_hbm, pg_hbm, gt_hbm, gr_hbm,
    x_ref, og_ref, gt_ref, gr_ref, tok_ref, cot_ref, cnt_ref, pick_ref, router_ref, win, wout,
    send, recv, gate_s, gate_r, pack_x, pack_d, pack_g, act_ref, pg_ref, slope_ref, head_s, head_r, tail_s, tail_r, ret_s, ret_r,
    term_s, term_r, sum_r, fin_r,
    in_sem, out_sem, d_ss, d_rs, g_ss, g_rs, x_ss, x_rs, y_ss, y_rs, z_ss, z_rs, h_ss, h_rs, r_ss, r_rs, b_ss, b_rs, t_ss, t_rs, s_ss, s_rs, f_ss, f_rs,
):
    me = lax.axis_index("expert")
    my_group = lax.axis_index("dp")
    toks, width = tok_ref.shape
    capacity = pick_ref.shape[1]
    hidden = win.shape[1]
    count = groups * capacity
    piece = send.shape[2]
    half = pack_x.shape[2]
    whole = 2 * half
    head = 2 * head_s.shape[2]
    back = ret_s.shape[2]
    chunk = term_s.shape[2]
    back_pieces = -(-(width + LANES) // back)

    barrier = pltpu.get_barrier_semaphore()
    for step in range(1, experts):
        pl.semaphore_signal(
            barrier, inc=1, device_id={"expert": lax.rem(me + step, experts)}, device_id_type=MESH
        )
    for step in range(1, groups):
        pl.semaphore_signal(
            barrier, inc=1, device_id={"dp": lax.rem(my_group + step, groups)}, device_id_type=MESH
        )
    loads = []
    for source, target in (
        (pick_hbm, pick_ref), (tok_hbm, tok_ref), (router_hbm, router_ref), (cnt_hbm, cnt_ref),
        (cot_hbm, cot_ref), (win_hbm, win), (wout_hbm, wout),
    ):
        loads.append(pltpu.make_async_copy(source, target, in_sem.at[len(loads)]))
    stores = []
    for source, target in (
        (x_ref, x_hbm), (og_ref, og_hbm), (act_ref, act_hbm), (pg_ref, pg_hbm), (gt_ref, gt_hbm), (gr_ref, gr_hbm)
    ):
        stores.append(pltpu.make_async_copy(source, target, out_sem.at[len(stores)]))
    load_pick, load_tok, load_router, load_cnt, load_cot, load_in, load_out = loads
    for load in loads[:5]:
        load.start()

    load_pick.wait()
    picks = pick_ref[...]
    owner = picks // toks
    place = picks - owner * toks
    codes = jnp.concatenate([owner, place], axis=1).astype(F32).astype(BF16)
    wide = experts * SEG
    spread = one_hot(iota((wide, experts), 0) // SEG == iota((wide, experts), 1))
    spread_codes = nn(spread, codes)
    held = spread_codes[:, :capacity] == me.astype(F32)
    spots = spread_codes[:, capacity:]
    first = jnp.min(jnp.where(held, spots, 1e6), axis=1, keepdims=True)
    last = jnp.max(jnp.where(held, spots, -1.0), axis=1, keepdims=True)
    last = jnp.where(last > first, last, -1.0)
    seat = iota((wide, toks), 0) % SEG
    token_id = iota((wide, toks), 1).astype(F32)
    hit = (token_id == jnp.where(seat % SLOT == 0, first, last)).astype(F32)
    late = seat % (2 * SLOT) >= SLOT
    take = jnp.concatenate([jnp.where(late, 0.0, hit), jnp.where(late, hit, 0.0)], axis=1)
    part_of = iota((wide, 2 * toks), 0) % SEG // (2 * SLOT)

    load_tok.wait()
    tok = tok_ref[...]
    load_cnt.wait()
    load_cot.wait()
    load_in.start()
    load_out.start()
    weight_row = jnp.maximum(cnt_ref[...], 1).astype(F32)
    diagonal = iota((toks, toks), 0) == iota((toks, toks), 1)
    weight = jnp.sum(jnp.where(diagonal, weight_row, 0.0), axis=1, keepdims=True)
    scaled = (cot_ref[...].astype(F32) * (1.0 / weight)).astype(BF16)

    pieces = SEG // (2 * SLOT)
    both = jnp.concatenate([tok, scaled], axis=0)
    total = jnp.zeros((wide, piece), F32)
    for part in range(pieces):
        low = part * piece
        high = min(width, low + piece)
        chosen = jnp.where(part_of == part, take, 0.0).astype(BF16)
        term = nn(chosen, both[:, low:high])
        if high - low < piece:
            term = jnp.concatenate([term, jnp.zeros((wide, piece - high + low), F32)], axis=1)
        total = total + term
    send[...] = total.astype(BF16).reshape(experts, SEG, piece)
    recv[pl.ds(me, 1)] = send[pl.ds(me, 1)]

    pl.semaphore_wait(barrier, experts - 1 + groups - 1)
    dispatch = exchange("expert", experts, me, lambda peer: send.at[peer], recv.at[me], d_ss, d_rs)

    load_router.wait()
    router = router_ref[...]
    stacked = jnp.concatenate(split3(router), axis=0).astype(BF16)
    parts = nt(stacked, tok)
    logits = parts[:experts] + parts[experts : 2 * experts] + parts[2 * experts :]
    raised = jnp.exp(logits - jnp.max(logits, axis=0, keepdims=True))
    prob = raised / jnp.sum(raised, axis=0, keepdims=True)
    padded = jnp.concatenate(
        split3(prob) + (jnp.zeros((LANES - 3 * experts, toks), F32),), axis=0
    )
    gate_s[...] = nt(hit.astype(BF16), padded.astype(BF16)).astype(BF16).reshape(experts, SEG, LANES)
    gate_r[pl.ds(me, 1)] = gate_s[pl.ds(me, 1)]
    send_gates = exchange("expert", experts, me, lambda peer: gate_s.at[peer], gate_r.at[me], g_ss, g_rs)

    mine = iota((experts, capacity), 0) == me
    owner_row = jnp.sum(jnp.where(mine, owner, 0), axis=0, keepdims=True)
    tall = 2 * capacity
    slot_row = iota((tall, capacity), 0) % capacity
    slot_col = iota((tall, capacity), 1)
    owner_col = jnp.sum(jnp.where(slot_row == slot_col, owner_row, 0), axis=1, keepdims=True)
    same = owner_col == owner_row
    rank_col = jnp.sum(jnp.where(same & (slot_col < slot_row), 1, 0), axis=1, keepdims=True)
    seat_c = iota((tall, wide), 1) % SEG
    is_dy = jnp.where(iota((tall, wide), 0) >= capacity, 1, 0)
    wanted = (iota((tall, wide), 1) // SEG == owner_col) & (
        seat_c % (2 * SLOT) == SLOT * is_dy + rank_col
    )
    blocks = [one_hot(wanted & (seat_c // (2 * SLOT) == part)) for part in range(pieces)]
    gate_block = one_hot(
        (iota((capacity, wide), 1) // SEG == owner_col[:capacity])
        & (iota((capacity, wide), 1) % SEG == rank_col[:capacity])
    )
    before = same[:capacity] & (slot_row[:capacity] < slot_col[:capacity])
    rank_row = jnp.sum(jnp.where(before, 1, 0), axis=0, keepdims=True)
    row_u = iota((wide, capacity), 0)
    from_owner = row_u // SEG == owner_row
    hit_turned = hit.T
    seat_turned = iota((toks, wide), 1) % SEG

    arrive(dispatch)
    rows_in = recv[...].reshape(wide, piece)
    packed = []
    for part in range(pieces):
        taken = min(width, (part + 1) * piece) - part * piece
        packed.append(nn(blocks[part], rows_in[:, :taken]))
    packed.append(jnp.zeros((tall, whole - width), F32))
    packed = jnp.concatenate(packed, axis=1)

    def folded(rows):
        return jnp.concatenate([rows[..., :half], rows[..., half:]], axis=-2).astype(BF16)

    def unfolded(pack):
        rows = pack[...].astype(F32)
        return jnp.concatenate([rows[:, :capacity], rows[:, capacity:]], axis=2).reshape(count, whole)

    pack_x[pl.ds(my_group, 1)] = folded(packed[:capacity])[None]
    gather_x = exchange(
        "dp", groups, my_group, lambda peer: pack_x.at[my_group], pack_x.at[my_group], x_ss, x_rs
    )
    pack_d[pl.ds(my_group, 1)] = folded(packed[capacity:])[None]
    gather_d = exchange(
        "dp", groups, my_group, lambda peer: pack_d.at[my_group], pack_d.at[my_group], y_ss, y_rs
    )
    arrive(send_gates)
    gate_rows = nn(gate_block, gate_r[...].reshape(wide, LANES))
    gate_rows = jnp.concatenate([gate_rows, jnp.zeros((capacity, LANES), F32)], axis=0)
    pack_g[pl.ds(my_group, 1)] = gate_rows.astype(BF16)[None]
    gather_g = exchange(
        "dp", groups, my_group, lambda peer: pack_g.at[my_group], pack_g.at[my_group], z_ss, z_rs
    )
    load_in.wait()
    load_out.wait()
    arrive(gather_x)

    x_rows = unfolded(pack_x)[:, :width].astype(BF16)
    x_ref[...] = x_rows
    stores[0].start()
    step_cols = min(hidden, 256)
    for tile in range(hidden // step_cols):
        cols = slice(tile * step_cols, (tile + 1) * step_cols)
        pre = nn(x_rows, win[:, cols])
        cdf = normal_cdf(pre)
        act_ref[:, cols] = (pre * cdf).astype(BF16)
        slope_ref[:, cols] = cdf + pre * jnp.exp(-0.5 * pre * pre) * 0.3989422804014327
    stores[2].start()

    arrive(gather_d)
    dy_wide = unfolded(pack_d)[:, :width]
    arrive(gather_g)
    gate_lanes = pack_g[...].astype(F32)[:, :capacity].reshape(count, LANES)
    lane = iota((count, LANES), 1)
    gate = jnp.sum(jnp.where(lane == me, gate_lanes, 0.0), axis=1, keepdims=True)
    dy_rows = dy_wide.astype(BF16)
    gate_part = jnp.zeros((count, 1), F32)
    for tile in range(hidden // step_cols):
        cols = slice(tile * step_cols, (tile + 1) * step_cols)
        back_act = nt(dy_rows, wout[cols, :])
        pg_ref[:, cols] = (gate * back_act * slope_ref[:, cols]).astype(BF16)
        gate_part = gate_part + jnp.sum(act_ref[:, cols].astype(F32) * back_act, axis=1, keepdims=True)
    stores[3].start()
    og_ref[...] = (gate * dy_wide).astype(BF16)
    stores[1].start()

    pre_grad = pg_ref[...]

    def row_columns(low, high):
        return [
            nt(pre_grad, win[start : min(high, start + 256), :]) for start in range(low, high, 256)
        ]

    def to_groups(columns, sent, kept, send_sem, recv_sem):
        rows = jnp.concatenate(columns, axis=1).reshape(groups, capacity, 2 * sent.shape[2])
        side = sent.shape[2]
        sent[...] = jnp.concatenate([rows[:, :, :side], rows[:, :, side:]], axis=1).astype(BF16)
        kept[pl.ds(my_group, 1)] = sent[pl.ds(my_group, 1)]
        return exchange(
            "dp", groups, my_group, lambda peer: sent.at[peer], kept.at[my_group], send_sem, recv_sem
        )

    head_sum = to_groups(row_columns(0, head), head_s, head_r, h_ss, h_rs)
    fold_row, fold_col = iota((LANES, LANES), 0), iota((LANES, LANES), 1)
    fold = one_hot((fold_row % experts == fold_col) & (fold_row < 3 * experts))
    row_prob = nn(gate_lanes.astype(BF16), fold)
    own_prob = jnp.sum(jnp.where(lane == me, row_prob, 0.0), axis=1, keepdims=True)
    logit_part = gate_part * row_prob * (jnp.where(lane == me, 1.0, 0.0) - own_prob)
    term = tn(
        jnp.concatenate(split3(logit_part), axis=0).astype(BF16),
        jnp.concatenate([x_rows, x_rows, x_rows], axis=0),
    )[:experts]
    for part in range(experts):
        low = part * chunk
        high = min(width, low + chunk)
        if high <= low:
            term_s[part] = jnp.zeros((experts, chunk), F32)
            continue
        value = term[:, low:high]
        if high - low < chunk:
            value = jnp.concatenate([value, jnp.zeros((experts, chunk - high + low), F32)], axis=1)
        term_s[part] = value
    term_r[pl.ds(me, 1)] = term_s[pl.ds(me, 1)]
    scatter = exchange("expert", experts, me, lambda peer: term_s.at[peer], term_r.at[me], t_ss, t_rs)

    g1, g2, g3 = split3(gate_part)
    tail = row_columns(head, width)
    tail.append(jnp.where(lane == 0, g1, jnp.where(lane == 1, g2, jnp.where(lane == 2, g3, 0.0))))
    spare = head + 2 * tail_s.shape[2] - width - LANES
    if spare:
        tail.append(jnp.zeros((count, spare), F32))
    tail_sum = to_groups(tail, tail_s, tail_r, r_ss, r_rs)

    def over_blocks(kept):
        summed = kept[0].astype(F32)
        for group in range(1, groups):
            summed = summed + kept[group].astype(F32)
        return [summed[:capacity], summed[capacity:]]

    arrive(scatter)
    term_sum = term_r[0]
    for part in range(1, experts):
        term_sum = term_sum + term_r[part]
    sum_r[pl.ds(my_group, 1)] = term_sum[None]
    over_dp = exchange("dp", groups, my_group, lambda peer: sum_r.at[my_group], sum_r.at[my_group], s_ss, s_rs)

    marks = [
        jnp.where(seat_turned // SLOT == part, hit_turned, 0.0).astype(BF16)
        for part in range(back_pieces)
    ]
    r1, r2, r3 = split3(router)
    near = jnp.concatenate([r1, r2, r1, r3, r1, r2], axis=0).astype(BF16)

    arrive(head_sum)
    row_sides = over_blocks(head_r)
    arrive(tail_sum)
    row_total = jnp.concatenate(row_sides + over_blocks(tail_r), axis=1)
    gate_total = jnp.sum(row_total[:, width : width + LANES], axis=1, keepdims=True)
    row_grad = jnp.concatenate(
        [
            row_total[:, :width],
            jnp.where(iota((capacity, LANES), 1) == me, gate_total, 0.0),
        ],
        axis=1,
    ).astype(BF16).astype(F32)
    returned = jnp.zeros((wide, back), F32)
    for part in range(back_pieces):
        low = part * back
        high = min(width + LANES, low + back)
        give = jnp.where(from_owner & (row_u % SEG == SLOT * part + rank_row), 1.0, 0.0)
        term = nn(give, row_grad[:, low:high])
        if high - low < back:
            term = jnp.concatenate([term, jnp.zeros((wide, back - high + low), F32)], axis=1)
        returned = returned + term
    ret_s[...] = returned.astype(BF16).reshape(experts, SEG, back)
    ret_r[pl.ds(me, 1)] = ret_s[pl.ds(me, 1)]
    give_back = exchange("expert", experts, me, lambda peer: ret_s.at[peer], ret_r.at[me], b_ss, b_rs)

    arrive(over_dp)
    final = sum_r[0]
    for group in range(1, groups):
        final = final + sum_r[group]
    fin_r[pl.ds(me, 1)] = final[None]
    spread_out = exchange("expert", experts, me, lambda peer: fin_r.at[me], fin_r.at[me], f_ss, f_rs)

    arrive(give_back)
    ret_rows = ret_r[...].reshape(wide, back)
    gate_low = width - (back_pieces - 1) * back
    prob_grad = nt(
        ret_rows[:, gate_low : gate_low + LANES].T, marks[back_pieces - 1]
    )[:experts]
    logit_grad = prob * (prob_grad - jnp.sum(prob * prob_grad, axis=0, keepdims=True))
    l1, l2, l3 = split3(logit_grad)
    left = jnp.concatenate([l1, l1, l2, l1, l3, l2], axis=0).astype(BF16)
    gt_wide = tn(left, near)
    for part in range(back_pieces):
        low = part * back
        high = min(width, low + back)
        expert_sum = nn(marks[part], ret_rows[:, : high - low])
        gt_ref[:, low:high] = (expert_sum + gt_wide[:, low:high]).astype(BF16)

    stores[4].start()

    arrive(spread_out)
    for part in range(experts):
        low = part * chunk
        high = min(width, low + chunk)
        if high > low:
            gr_ref[:, low:high] = fin_r[part][:, : high - low]
    stores[5].start()
    for store in stores:
        store.wait()
    for copies in (dispatch, send_gates, gather_x, gather_d, gather_g, head_sum, tail_sum, give_back, scatter, over_dp, spread_out):
        for copy in copies:
            copy.wait_send()


def weight_kernel(
    x_hbm, og_hbm, act_hbm, pg_hbm, gt_in, gr_in, gt_hbm, gin_hbm, gout_hbm, gr_hbm,
    x_ref, og_ref, act_ref, pg_ref, gt_ref, gr_ref, gin_ref, gout_ref, in_sem, out_sem,
):
    loads = []
    for source, target in (
        (x_hbm, x_ref), (pg_hbm, pg_ref), (act_hbm, act_ref), (og_hbm, og_ref), (gt_in, gt_ref), (gr_in, gr_ref)
    ):
        loads.append(pltpu.make_async_copy(source, target, in_sem.at[len(loads)]))
        loads[-1].start()
    stores = []

    def product(left, right, held, target):
        rows = held.shape[0]
        for low in range(0, rows, 256):
            span = slice(low, min(rows, low + 256))
            held[span, :] = tn(left[:, span], right[...]).astype(BF16)
            stores.append(pltpu.make_async_copy(held.at[span], target.at[0, span], out_sem.at[len(stores)]))
            stores[-1].start()

    loads[0].wait()
    loads[1].wait()
    product(x_ref, pg_ref, gin_ref, gin_hbm)
    for load, held, target in ((loads[4], gt_ref, gt_hbm), (loads[5], gr_ref, gr_hbm)):
        load.wait()
        stores.append(pltpu.make_async_copy(held, target, out_sem.at[len(stores)]))
        stores[-1].start()
    loads[2].wait()
    loads[3].wait()
    product(act_ref, og_ref, gout_ref, gout_hbm)
    for store in stores:
        store.wait()


def shards(experts, groups, tokens, cotangent, counts, picks, router, w_in, w_out):
    toks, width = tokens.shape
    capacity = picks.shape[2]
    hidden = w_in.shape[2]
    count = groups * capacity
    tiles = -(-width // LANES)
    pieces = SEG // (2 * SLOT)
    piece = LANES * -(-tiles // pieces)
    half = LANES * -(-(tiles + 1) // 2)
    back = LANES * -(-(tiles + 1) // (SEG // SLOT))
    head = LANES * ((tiles + 1) * 2 // 7)
    tail = half - head
    chunk = LANES * -(-tiles // experts)
    hbm = pl.BlockSpec(memory_space=pltpu.HBM)
    dma = pltpu.SemaphoreType.DMA
    over_e, over_g = dma((experts,)), dma((groups,))
    row_scratch = [
        pltpu.VMEM((count, width), BF16),
        pltpu.VMEM((count, width), BF16),
    ]
    results = pl.pallas_call(
        functools.partial(route_kernel, experts, groups),
        out_shape=(
            jax.ShapeDtypeStruct((count, width), BF16),
            jax.ShapeDtypeStruct((count, width), BF16),
            jax.ShapeDtypeStruct((count, hidden), BF16),
            jax.ShapeDtypeStruct((count, hidden), BF16),
            jax.ShapeDtypeStruct((toks, width), BF16),
            jax.ShapeDtypeStruct((experts, width), F32),
        ),
        in_specs=[hbm] * 7,
        out_specs=(hbm,) * 6,
        scratch_shapes=row_scratch
        + [
            pltpu.VMEM((toks, width), BF16),
            pltpu.VMEM((experts, width), F32),
            pltpu.VMEM((toks, width), BF16),
            pltpu.VMEM((toks, width), BF16),
            pltpu.VMEM((1, toks), jnp.int32),
            pltpu.VMEM((experts, capacity), jnp.int32),
            pltpu.VMEM((experts, width), F32),
            pltpu.VMEM((width, hidden), BF16),
            pltpu.VMEM((hidden, width), BF16),
            pltpu.VMEM((experts, SEG, piece), BF16),
            pltpu.VMEM((experts, SEG, piece), BF16),
            pltpu.VMEM((experts, SEG, LANES), BF16),
            pltpu.VMEM((experts, SEG, LANES), BF16),
            pltpu.VMEM((groups, 2 * capacity, half), BF16),
            pltpu.VMEM((groups, 2 * capacity, half), BF16),
            pltpu.VMEM((groups, 2 * capacity, LANES), BF16),
            pltpu.VMEM((count, hidden), BF16),
            pltpu.VMEM((count, hidden), BF16),
            pltpu.VMEM((count, hidden), F32),
            pltpu.VMEM((groups, 2 * capacity, head), BF16),
            pltpu.VMEM((groups, 2 * capacity, head), BF16),
            pltpu.VMEM((groups, 2 * capacity, tail), BF16),
            pltpu.VMEM((groups, 2 * capacity, tail), BF16),
            pltpu.VMEM((experts, SEG, back), BF16),
            pltpu.VMEM((experts, SEG, back), BF16),
            pltpu.VMEM((experts, experts, chunk), F32),
            pltpu.VMEM((experts, experts, chunk), F32),
            pltpu.VMEM((groups, experts, chunk), F32),
            pltpu.VMEM((experts, experts, chunk), F32),
            dma((7,)),
            dma((6,)),
            over_e, over_e,
            over_e, over_e,
            over_g, over_g,
            over_g, over_g,
            over_g, over_g,
            over_g, over_g,
            over_g, over_g,
            over_e, over_e,
            over_e, over_e,
            over_g, over_g,
            over_e, over_e,
        ],
        compiler_params=pltpu.CompilerParams(
            collective_id=0, has_side_effects=True, vmem_limit_bytes=58 * 1024 * 1024
        ),
        name="route",
    )(tokens, cotangent, counts.reshape(1, toks), picks[0], router.T, w_in[0], w_out[0])

    grad_tokens, grad_in, grad_out, grad_router = pl.pallas_call(
        weight_kernel,
        out_shape=(
            jax.ShapeDtypeStruct((toks, width), BF16),
            jax.ShapeDtypeStruct((1, width, hidden), BF16),
            jax.ShapeDtypeStruct((1, hidden, width), BF16),
            jax.ShapeDtypeStruct((experts, width), F32),
        ),
        in_specs=[hbm] * 6,
        out_specs=(hbm,) * 4,
        scratch_shapes=row_scratch
        + [
            pltpu.VMEM((count, hidden), BF16),
            pltpu.VMEM((count, hidden), BF16),
            pltpu.VMEM((toks, width), BF16),
            pltpu.VMEM((experts, width), F32),
            pltpu.VMEM((width, hidden), BF16),
            pltpu.VMEM((hidden, width), BF16),
            dma((6,)),
            dma((-(-width // 256) + -(-hidden // 256) + 2,)),
        ],
        compiler_params=pltpu.CompilerParams(vmem_limit_bytes=58 * 1024 * 1024),
        name="weight_grads",
    )(*results)
    return grad_tokens, grad_in, grad_out, grad_router.T


def solution(mesh):
    placed = (
        P(("dp", "expert"), None),
        P(("dp", "expert"), None),
        P(("dp", "expert")),
        P("dp", None, None),
        P(),
        P("expert", None, "dp"),
        P("expert", "dp", None),
    )
    return jax.shard_map(
        functools.partial(shards, mesh.shape["expert"], mesh.shape["dp"]),
        mesh=mesh,
        in_specs=placed,
        out_specs=(
            P(("dp", "expert"), None),
            P("expert", None, "dp"),
            P("expert", "dp", None),
            P(),
        ),
        check_vma=False,
    )
```
